768 devices in a mesh: grid: 96 (over z, x, core), mesh: 8 (over y).
Axes of the slice: x: 4, y: 8, z: 12, core: 2. Of those that a mesh axis runs over, the one named last changes fastest.
Arguments:
- grid_vars: bfloat16 [196608, 227], P(('grid', 'mesh')), may hold values from -6 to 6
- mesh_init: bfloat16 [98304, 512], P(('grid', 'mesh')), may hold values from -6 to 6
- w_embed: bfloat16 [227, 512], replicated, may hold values from -0.375 to 0.375
- w_send: bfloat16 [512, 512], replicated, may hold values from -0.25 to 0.25
- w_node: bfloat16 [512, 512], replicated, may hold values from -0.25 to 0.25
- node_gain: float32 [512], replicated, may hold values from 0.5 to 2
- w_proc_send: bfloat16 [512, 512], replicated, may hold values from -0.25 to 0.25
- w_proc_recv: bfloat16 [512, 512], replicated, may hold values from -0.25 to 0.25
- w_proc_out: bfloat16 [512, 512], replicated, may hold values from -0.25 to 0.25
- w_dec_send: bfloat16 [512, 512], replicated, may hold values from -0.25 to 0.25
- w_dec_out: bfloat16 [512, 227], replicated, may hold values from -0.25 to 0.25
- enc_src: int32 [294912], P(('grid', 'mesh')), may hold values from 0 to 255
- enc_dst: int32 [294912], P(('grid', 'mesh')), may hold values from 0 to 3071
- proc_src: int32 [786432], P(('grid', 'mesh')), may hold values from 0 to 3071
- proc_dst: int32 [786432], P(('grid', 'mesh')), may hold values from 0 to 127
- dec_src: int32 [589824], P(('grid', 'mesh')), may hold values from 0 to 3071
- dec_dst: int32 [589824], P(('grid', 'mesh')), may hold values from 0 to 255
Outputs:
- next_vars: bfloat16 [196608, 227], P(('grid', 'mesh'))
The draws below stay inside these ranges and needn't reach their ends.
Inputs may be any that keep to these rules, and one draw needn't show every extreme that they name: `enc_src`: local grid node numbers of the sending device. `enc_dst`: neighbourhood codes: band offset times 8 * 128 plus the node number within the band group. `proc_src`: neighbourhood codes as for enc_dst. `proc_dst`: local mesh node numbers of the receiving device. `dec_src`: neighbourhood codes as for enc_dst. `dec_dst`: local grid node numbers of the receiving device.
All inputs are finite; a program needn't handle non-finite values.
Results may differ from the reference program's by a relative error of at most 0.012.
Values may be sent and summed in bfloat16 or wider, within the bound.
No kernel may reach another device: no remote copies, remote signals or barrier semaphores. Data moves between devices by JAX's collectives and lax.ppermute only.
A program may use at most 32 MiB of HBM per device.

```python
import math
import jax
import jax.numpy as jnp
from jax import lax

D = 512
VARS = 227
GRID_DEV = 256
MESH_DEV = 128
HOOD = 3072
GRID = 196608
MESH = 98304
ENC_EDGES = 294912
PROC_EDGES = 786432
DEC_EDGES = 589824
N_GRID = 96
N_MESH = 8


def place_ends(array, stream_key, least, top_value):
    shape = array.shape
    spot = [jax.random.randint(jax.random.fold_in(stream_key, axis), (), 0, shape[axis]) for axis in range(len(shape))]
    array = array.at[tuple(spot)].set(least)
    longest = shape.index(max(shape))
    spot[longest] = (spot[longest] + 1) % shape[longest]
    return array.at[tuple(spot)].set(top_value)


def steps_of(rng, extent, cuts, smallest, largest):
    def one(axis_at, shards_of):
        draws = jax.random.uniform(jax.random.fold_in(jax.random.fold_in(rng, 6), axis_at), (shards_of,), jnp.float32, smallest / len(cuts), largest / len(cuts))
        return jnp.repeat(jnp.exp(draws), extent[axis_at] // shards_of).reshape((-1,) + (1,) * (len(extent) - axis_at - 1))

    gain = one(*cuts[0])
    for cut in cuts[1:]:
        gain = gain * one(*cut)
    return gain


def normal_values(stream_key, extent, width, reach, pieces=(), kind=jnp.bfloat16):
    result = jax.random.normal(stream_key, extent, jnp.float32) * width
    if len(pieces) > 0:
        result = steps_of(stream_key, extent, pieces, -0.22, 0.18) * result
    return jnp.clip(result, min=-reach, max=reach).astype(kind)


def setup_inputs(seed: int = 0) -> dict:
    arg_keys = jax.random.split(jax.random.key(seed), 18)
    grid_vars = normal_values(arg_keys[0], (GRID, VARS), 1.0, 6.0, ((0, 768),))
    mesh_init = normal_values(arg_keys[1], (MESH, D), 1.0, 6.0, ((0, 768),))
    w_embed = normal_values(arg_keys[2], (VARS, D), VARS ** -0.5, 0.375)
    w_send = normal_values(arg_keys[3], (D, D), D ** -0.5, 0.25)
    w_node = normal_values(arg_keys[4], (D, D), D ** -0.5, 0.25)
    node_gain = jnp.clip(jnp.exp(jax.random.uniform(arg_keys[5], (D,), jnp.float32, math.log(0.5), math.log(2.0))), 0.5, 2.0)
    w_proc_send = normal_values(arg_keys[6], (D, D), D ** -0.5, 0.25)
    w_proc_recv = normal_values(arg_keys[7], (D, D), D ** -0.5, 0.25)
    w_proc_out = normal_values(arg_keys[8], (D, D), D ** -0.5, 0.25)
    w_dec_send = normal_values(arg_keys[9], (D, D), D ** -0.5, 0.25)
    w_dec_out = normal_values(arg_keys[10], (D, VARS), D ** -0.5, 0.25)
    enc_src = place_ends(jax.random.randint(arg_keys[11], (ENC_EDGES,), 0, GRID_DEV), jax.random.fold_in(arg_keys[11], 1), 0, GRID_DEV - 1).astype(jnp.int32)
    enc_dst = place_ends(jax.random.randint(arg_keys[12], (ENC_EDGES,), 0, HOOD), jax.random.fold_in(arg_keys[12], 1), 0, HOOD - 1).astype(jnp.int32)
    proc_src = place_ends(jax.random.randint(arg_keys[13], (PROC_EDGES,), 0, HOOD), jax.random.fold_in(arg_keys[13], 1), 0, HOOD - 1).astype(jnp.int32)
    proc_dst = place_ends(jax.random.randint(arg_keys[14], (PROC_EDGES,), 0, MESH_DEV), jax.random.fold_in(arg_keys[14], 1), 0, MESH_DEV - 1).astype(jnp.int32)
    dec_src = place_ends(jax.random.randint(arg_keys[15], (DEC_EDGES,), 0, HOOD), jax.random.fold_in(arg_keys[15], 1), 0, HOOD - 1).astype(jnp.int32)
    dec_dst = place_ends(jax.random.randint(arg_keys[16], (DEC_EDGES,), 0, GRID_DEV), jax.random.fold_in(arg_keys[16], 1), 0, GRID_DEV - 1).astype(jnp.int32)
    return {"grid_vars": grid_vars, "mesh_init": mesh_init, "w_embed": w_embed, "w_send": w_send, "w_node": w_node, "node_gain": node_gain, "w_proc_send": w_proc_send, "w_proc_recv": w_proc_recv, "w_proc_out": w_proc_out, "w_dec_send": w_dec_send, "w_dec_out": w_dec_out, "enc_src": enc_src, "enc_dst": enc_dst, "proc_src": proc_src, "proc_dst": proc_dst, "dec_src": dec_src, "dec_dst": dec_dst}


def rms_rows(values):
    return values * lax.rsqrt(lax.optimization_barrier(jnp.mean(values * values, axis=-1, keepdims=True)) + 1e-05)

def codes_to_nodes(codes, band_nodes):
    bands = jnp.arange(N_GRID, dtype=jnp.int32)[:, None, None]
    target = bands + codes // band_nodes - 1
    valid = (target >= 0) & (target < N_GRID)
    index = jnp.where(valid, target * band_nodes + codes % band_nodes, 0).astype(jnp.int32)
    return (index, valid)

def local_first(count):
    bands = jnp.arange(N_GRID, dtype=jnp.int32)[:, None, None]
    patches = jnp.arange(N_MESH, dtype=jnp.int32)[None, :, None]
    return (bands * N_MESH + patches) * count

def reference(grid_vars, mesh_init, w_embed, w_send, w_node, node_gain, w_proc_send, w_proc_recv, w_proc_out, w_dec_send, w_dec_out, enc_src, enc_dst, proc_src, proc_dst, dec_src, dec_dst):
    band_nodes = N_MESH * MESH_DEV
    grid_lat = jax.nn.silu(jnp.dot(grid_vars, w_embed, preferred_element_type=jnp.float32)).astype(jnp.bfloat16)
    enc_out = jax.nn.silu(jnp.dot(grid_lat, w_send, preferred_element_type=jnp.float32)).astype(jnp.bfloat16)
    senders = (local_first(GRID_DEV) + enc_src.reshape(N_GRID, N_MESH, -1)).reshape(-1)
    index, valid = codes_to_nodes(enc_dst.reshape(N_GRID, N_MESH, -1), band_nodes)
    target = jnp.where(valid, index, MESH).reshape(-1)
    enc_agg = jax.ops.segment_sum(enc_out[senders].astype(jnp.float32), target, num_segments=MESH + 1)[:MESH]
    node_in = jax.nn.silu(rms_rows(enc_agg) * node_gain).astype(jnp.bfloat16)
    mesh_one = (mesh_init.astype(jnp.float32) + jnp.dot(node_in, w_node, preferred_element_type=jnp.float32)).astype(jnp.bfloat16)
    send_index, send_valid = codes_to_nodes(proc_src.reshape(N_GRID, N_MESH, -1), band_nodes)
    recv_index = (local_first(MESH_DEV) + proc_dst.reshape(N_GRID, N_MESH, -1)).reshape(-1)
    send_proj = jnp.dot(mesh_one[send_index.reshape(-1)], w_proc_send, preferred_element_type=jnp.float32)
    recv_proj = jnp.dot(mesh_one, w_proc_recv, preferred_element_type=jnp.float32)[recv_index]
    proc_msg = (jax.nn.silu(send_proj + recv_proj) * send_valid.reshape(-1, 1).astype(jnp.float32)).astype(jnp.bfloat16)
    proc_agg = jax.ops.segment_sum(proc_msg.astype(jnp.float32), recv_index, num_segments=MESH)
    proc_norm = rms_rows(proc_agg).astype(jnp.bfloat16)
    mesh_two = (mesh_one.astype(jnp.float32) + jnp.dot(proc_norm, w_proc_out, preferred_element_type=jnp.float32)).astype(jnp.bfloat16)
    dec_out = jax.nn.silu(jnp.dot(mesh_two, w_dec_send, preferred_element_type=jnp.float32)).astype(jnp.bfloat16)
    dec_index, dec_valid = codes_to_nodes(dec_src.reshape(N_GRID, N_MESH, -1), band_nodes)
    dec_msg = dec_out[dec_index.reshape(-1)].astype(jnp.float32) * dec_valid.reshape(-1, 1).astype(jnp.float32)
    receivers = (local_first(GRID_DEV) + dec_dst.reshape(N_GRID, N_MESH, -1)).reshape(-1)
    dec_agg = jax.ops.segment_sum(dec_msg, receivers, num_segments=GRID)
    dec_norm = rms_rows(dec_agg).astype(jnp.bfloat16)
    return (grid_vars.astype(jnp.float32) + jnp.dot(dec_norm, w_dec_out, preferred_element_type=jnp.float32)).astype(jnp.bfloat16)
```

```python
import functools

import jax
import jax.numpy as jnp
from jax import lax
from jax.experimental import pallas as pl
from jax.experimental.pallas import tpu as pltpu
from jax.sharding import PartitionSpec as P

LANES = 128
VMEM_BYTES = 56 * 1024 * 1024


def silu(v):
    return v * (0.5 + 0.5 * jnp.tanh(0.5 * v))


def rms(v):
    return v * lax.rsqrt(jnp.mean(v * v, axis=-1, keepdims=True) + 1e-05)


def mm(a, b):
    return jnp.dot(a, b, preferred_element_type=jnp.float32)


def mm_nt(a, b):
    return lax.dot_general(a, b, (((1,), (1,)), ((), ())), preferred_element_type=jnp.float32)


def hot_by_row(keys, count):
    spots = lax.broadcasted_iota(jnp.int32, (count, keys.shape[1]), 0)
    return jnp.where(spots == keys, 1.0, 0.0).astype(jnp.bfloat16)


def columns_of(row):
    return jnp.transpose(jnp.broadcast_to(row, (LANES, LANES)))


def hot_by_column(spread, count):
    lanes = lax.broadcasted_iota(jnp.int32, (LANES, LANES), 1)
    parts = [
        jnp.where(spread == lanes + LANES * k, 1.0, 0.0).astype(jnp.bfloat16)
        for k in range(count // LANES)
    ]
    return jnp.concatenate(parts, axis=1)


def band_sums(pick, buf, w_embed, w_send, out, rows, edges):
    grid_rows = rows - 16
    chunks = edges // LANES
    nodes = out.shape[0]
    patches = buf.shape[0] // rows

    def device(s, carry):
        base = pl.multiple_of(s * rows, 16)
        lat = silu(mm(buf[pl.ds(base, grid_rows), :], w_embed[...])).astype(jnp.bfloat16)
        sent = silu(mm(lat, w_send[...])).astype(jnp.bfloat16)
        notes = buf[pl.ds(pl.multiple_of(base + grid_rows, 16), 16), :LANES]
        notes = notes.astype(jnp.float32).astype(jnp.int32)
        src = notes[0:chunks]
        high = notes[chunks : 2 * chunks]
        low = notes[2 * chunks : 3 * chunks]
        key = jnp.where(
            high // patches == pick, (high % patches) * LANES + low, -1
        )
        to = jnp.concatenate([hot_by_row(key[j : j + 1], nodes) for j in range(chunks)], axis=1)
        frm = jnp.concatenate([hot_by_row(src[j : j + 1], grid_rows) for j in range(chunks)], axis=1)
        counts = mm_nt(to, frm).astype(jnp.bfloat16)
        out[...] += mm(counts, sent)
        return carry

    lax.fori_loop(0, patches, device, 0)


def enc_first(pick, buf, w_embed, w_send, out, *, rows, edges):
    out[...] = jnp.zeros_like(out)
    band_sums(pick[0], buf, w_embed, w_send, out, rows, edges)


def enc_more(pick, buf, w_embed, w_send, acc, out, *, rows, edges):
    out[...] = acc[...]
    band_sums(pick[0], buf, w_embed, w_send, out, rows, edges)


def enc_last(pick, buf, w_embed, w_send, acc, init, gain, w_node, out, total, *, rows, edges):
    total[...] = acc[...]
    band_sums(pick[0], buf, w_embed, w_send, total, rows, edges)
    step = 256

    def block(i, carry):
        here = pl.ds(pl.multiple_of(i * step, step), step)
        node_in = silu(rms(total[here, :]) * gain[...]).astype(jnp.bfloat16)
        fresh = init[here, :].astype(jnp.float32) + mm(node_in, w_node[...])
        out[here, :] = fresh.astype(jnp.bfloat16)
        return carry

    lax.fori_loop(0, out.shape[0] // step, block, 0)


def picked_rows(pick, src, nodes, put):
    count = nodes.shape[0]
    for j in range(src.shape[0]):
        code = src[j : j + 1, :]
        key = jnp.where(code // count == pick, code % count, -1)
        put(j, mm(hot_by_column(columns_of(key), count), nodes[...]))


def proc_first(pick, src, nodes, out):
    def put(j, rows):
        out[LANES * j : LANES * (j + 1), :] = rows.astype(jnp.bfloat16)

    picked_rows(pick[0], src, nodes, put)


def proc_more(pick, src, nodes, acc, out):
    def put(j, rows):
        at = slice(LANES * j, LANES * (j + 1))
        out[at, :] = acc[at, :] + rows.astype(jnp.bfloat16)

    picked_rows(pick[0], src, nodes, put)


def proc_last(
    pick, src, dst, nodes, acc, own, w_ps, w_pr, w_po, w_ds, out, *, last_band, band_nodes
):
    recv = mm(own[...], w_pr[...])
    top = recv.astype(jnp.bfloat16)
    rest = (recv - top.astype(jnp.float32)).astype(jnp.bfloat16)
    recv_pair = jnp.concatenate([top, rest], axis=0)
    total = jnp.zeros(own.shape, jnp.float32)
    count = nodes.shape[0]
    band = pick[1]
    for j in range(src.shape[0]):
        at = slice(LANES * j, LANES * (j + 1))
        code = src[j : j + 1, :]
        to = dst[j : j + 1, :]
        key = jnp.where(code // count == pick[0], code % count, -1)
        rows = mm(hot_by_column(columns_of(key), count), nodes[...]).astype(jnp.bfloat16)
        rows = acc[at, :] + rows
        one = hot_by_column(columns_of(to), LANES)
        recv_rows = mm(jnp.concatenate([one, one], axis=1), recv_pair)
        msg = silu(mm(rows, w_ps[...]) + recv_rows).astype(jnp.bfloat16)
        target = band + code // band_nodes - 1
        valid = (target >= 0) & (target <= last_band)
        total += mm(hot_by_row(jnp.where(valid, to, -1), LANES), msg)
    norm = rms(total).astype(jnp.bfloat16)
    two = (own[...].astype(jnp.float32) + mm(norm, w_po[...])).astype(jnp.bfloat16)
    out[...] = silu(mm(two, w_ds[...])).astype(jnp.bfloat16)


def dec_counts(keys, dst, out):
    chunks = dst.shape[0]
    grid_rows = out.shape[0]
    nodes = out.shape[1] // 3
    to = jnp.concatenate([hot_by_row(dst[j : j + 1, :], grid_rows) for j in range(chunks)], axis=1)
    half = nodes // 2
    for k in range(6):
        first = (k // 2) * chunks
        frm = jnp.concatenate(
            [
                hot_by_row(keys[first + j : first + j + 1, :] - (k % 2) * half, half)
                for j in range(chunks)
            ],
            axis=1,
        )
        out[:, k * half : (k + 1) * half] = mm_nt(to, frm).astype(jnp.bfloat16)


def dec_last(counts, a, b, c, d, e, f, grid_vars, w_out, out):
    half = a.shape[0]
    total = jnp.zeros((counts.shape[0], a.shape[1]), jnp.float32)
    for k, part in enumerate((a, b, c, d, e, f)):
        total += mm(counts[:, k * half : (k + 1) * half], part[...])
    norm = rms(total).astype(jnp.bfloat16)
    out[...] = (grid_vars[...].astype(jnp.float32) + mm(norm, w_out[...])).astype(jnp.bfloat16)


def call(body, out, *args, scalars=0, scratch=(), flops=0, **static):
    vmem = pl.BlockSpec(memory_space=pltpu.VMEM)
    smem = pl.BlockSpec(memory_space=pltpu.SMEM)
    moved = sum(a.size * a.dtype.itemsize for a in args) + out.size * out.dtype.itemsize
    return pl.pallas_call(
        functools.partial(body, **static),
        out_shape=out,
        in_specs=[smem] * scalars + [vmem] * (len(args) - scalars),
        out_specs=vmem,
        scratch_shapes=list(scratch),
        compiler_params=pltpu.CompilerParams(vmem_limit_bytes=VMEM_BYTES),
        cost_estimate=pl.CostEstimate(flops=flops, bytes_accessed=moved, transcendentals=0),
        name=body.__name__,
    )(*args)


def pair_groups(bands, patches, step):
    groups = []
    for b in range(bands):
        for p in range(patches):
            if (p + b) % 2 == 0:
                q = (p + 1) % patches if step == 0 else (p - 1) % patches
                groups.append([b * patches + p, b * patches + q])
    return groups


def shards(
    bands,
    patches,
    grid_vars,
    mesh_init,
    w_embed,
    w_send,
    w_node,
    node_gain,
    w_proc_send,
    w_proc_recv,
    w_proc_out,
    w_dec_send,
    w_dec_out,
    enc_src,
    enc_dst,
    proc_src,
    proc_dst,
    dec_src,
    dec_dst,
):
    f32, bf16 = jnp.float32, jnp.bfloat16
    shape = jax.ShapeDtypeStruct
    mine, width = mesh_init.shape
    band_nodes = patches * mine
    grid_rows, columns = grid_vars.shape
    edges = enc_src.shape[0]
    chunks = edges // LANES
    band = lax.axis_index("grid").astype(jnp.int32)
    patch = lax.axis_index("mesh").astype(jnp.int32)
    odd = band % 2
    far = 2 * odd
    near = 2 - far
    far_pairs = [(i, i + 1) for i in range(1, bands - 1, 2)]
    far_pairs += [(j, i) for i, j in far_pairs]
    near_pairs = [(i, i + 1) for i in range(0, bands - 1, 2)]
    near_pairs += [(j, i) for i, j in near_pairs]

    def over_far(block):
        return lax.ppermute(block, "grid", far_pairs)

    def over_near(block):
        return lax.ppermute(block, "grid", near_pairs)

    init_band = lax.all_gather(mesh_init, "mesh", axis=0, tiled=True)

    notes = jnp.concatenate([enc_src, enc_dst // LANES, enc_dst % LANES]).reshape(3 * chunks, LANES)
    notes = jnp.pad(notes.astype(bf16), ((0, 16 - 3 * chunks), (0, columns - LANES)))
    load = jnp.concatenate([grid_vars, notes], axis=0)
    rows = grid_rows + 16
    own = lax.all_gather(load, "mesh", axis=0, tiled=True)
    far_load = over_far(own)
    near_load = over_near(own)

    def scalar(v):
        return jnp.reshape(v, (1,)).astype(jnp.int32)

    enc_flops = 2 * patches * (
        grid_rows * width * (2 * LANES + width)
        + band_nodes * grid_rows * (edges + width)
    )
    acc_shape = shape((band_nodes, width), f32)
    enc = dict(rows=rows, edges=edges, scalars=1, flops=enc_flops)
    acc = call(enc_first, acc_shape, scalar(1), own, w_embed, w_send, **enc)
    acc = call(enc_more, acc_shape, scalar(2 - near), near_load, w_embed, w_send, acc, **enc)
    one = call(
        enc_last,
        shape((band_nodes, width), bf16),
        scalar(2 - far),
        far_load,
        w_embed,
        w_send,
        acc,
        init_band,
        node_gain.reshape(1, width),
        w_node,
        scratch=[pltpu.VMEM((band_nodes, width), f32)],
        **enc,
    )

    far_one = over_far(one)
    near_one = over_near(one)
    own_one = lax.dynamic_slice_in_dim(one, patch * mine, mine, 0)
    src = proc_src.reshape(-1, LANES)
    dst = proc_dst.reshape(-1, LANES)
    proc_edges = proc_src.shape[0]
    pick_flops = 2 * proc_edges * band_nodes * width
    pick_shape = shape((proc_edges, width), bf16)
    got = call(proc_first, pick_shape, scalar(1), src, one, scalars=1, flops=pick_flops)

    code_band = dec_src // band_nodes
    block = (dec_src // mine) % patches
    within = dec_src % mine
    dec_keys = []
    for wanted, parity in ((1, 0), (near, 1), (far, 1)):
        second = (patch + band + parity) % 2
        rel = (block - patch) * (1 - 2 * second)
        turn = (rel + 2) % patches
        spot = jnp.where(turn < 4, turn ^ 2, turn) ^ (3 * second)
        dec_keys.append(jnp.where(code_band == wanted, spot * mine + within, -band_nodes))
    dec_keys = jnp.concatenate(dec_keys).reshape(-1, LANES)
    dec_edges = dec_src.shape[0]
    counts = call(
        dec_counts,
        shape((grid_rows, 3 * band_nodes), bf16),
        dec_keys,
        dec_dst.reshape(-1, LANES),
        flops=6 * grid_rows * band_nodes * dec_edges,
    )

    got = call(proc_more, pick_shape, scalar(near), src, near_one, got, scalars=1, flops=pick_flops)
    sent = call(
        proc_last,
        shape((mine, width), bf16),
        jnp.stack([far, band]).astype(jnp.int32),
        src,
        dst,
        far_one,
        got,
        own_one,
        w_proc_send,
        w_proc_recv,
        w_proc_out,
        w_dec_send,
        scalars=1,
        flops=pick_flops + 2 * proc_edges * width * (width + 3 * LANES),
        last_band=bands - 1,
        band_nodes=band_nodes,
    )

    groups = [pair_groups(bands, patches, step) for step in (0, 1)]

    def meet(rows_here, step):
        return lax.all_gather(
            rows_here, ("grid", "mesh"), axis=0, tiled=True, axis_index_groups=groups[step]
        )

    second = (patch + band) % 2

    def partner_half(both):
        size = both.shape[0] // 2
        return lax.dynamic_slice_in_dim(both, (1 - second) * size, size, 0)

    four = meet(meet(sent, 0), 1)
    far_four = over_far(four)
    near_four = over_near(four)
    rest = meet(partner_half(meet(partner_half(four), 0)), 1)
    far_rest = over_far(rest)
    near_rest = over_near(rest)
    return call(
        dec_last,
        shape((grid_rows, columns), bf16),
        counts,
        four,
        rest,
        near_four,
        near_rest,
        far_four,
        far_rest,
        grid_vars,
        w_dec_out,
        flops=6 * grid_rows * band_nodes * width,
    )


def solution(mesh):
    spread = P(("grid", "mesh"), None)
    edge = P(("grid", "mesh"))
    in_specs = (spread, spread) + (P(),) * 9 + (edge,) * 6
    body = functools.partial(shards, mesh.shape["grid"], mesh.shape["mesh"])
    return jax.shard_map(body, mesh=mesh, in_specs=in_specs, out_specs=spread, check_vma=False)
```

```python
import functools

import jax
import jax.numpy as jnp
from jax import lax
from jax.experimental import pallas as pl
from jax.experimental.pallas import tpu as pltpu
from jax.sharding import PartitionSpec as P

LANES = 128
MIB = 1024 * 1024


def silu(v):
    return v * (0.5 + 0.5 * jnp.tanh(0.5 * v))


def rms(v):
    return v * lax.rsqrt(jnp.mean(v * v, axis=-1, keepdims=True) + 1e-05)


def mm(a, b):
    return jnp.dot(a, b, preferred_element_type=jnp.float32)


def mm_tn(a, b):
    return lax.dot_general(a, b, (((0,), (0,)), ((), ())), preferred_element_type=jnp.float32)


def mm_nt(a, b):
    return lax.dot_general(a, b, (((1,), (1,)), ((), ())), preferred_element_type=jnp.float32)


def hot_by_row(keys, count):
    spots = lax.broadcasted_iota(jnp.int16, (count, keys.shape[1]), 0)
    one, none = jnp.bfloat16(1), jnp.bfloat16(0)
    return jnp.where(spots == keys.astype(jnp.int16), one, none)


def columns_of(row):
    return jnp.transpose(jnp.broadcast_to(row, (LANES, LANES)))


def hot_by_column(spread, count):
    lanes = lax.broadcasted_iota(jnp.int32, (LANES, LANES), 1)
    parts = [
        jnp.where(spread == lanes + LANES * k, 1.0, 0.0).astype(jnp.bfloat16)
        for k in range(count // LANES)
    ]
    return jnp.concatenate(parts, axis=1)


def side(parts):
    return jnp.concatenate(parts, axis=1)


def notes_of(buf, s, columns, count):
    start = columns // 16 * 16
    notes = buf[s, start:, :].astype(jnp.float32).astype(jnp.int32)
    skip = columns - start

    def piece(k):
        row, lane = skip + k // 2, LANES * (k % 2)
        return notes[row : row + 1, lane : lane + LANES]

    return [piece(k) for k in range(count)]


def band_sums(pick, buf, w_embed, w_send, acc, out, lat, sent, counts, chunks):
    patches, _, grid_rows = buf.shape
    columns = w_embed.shape[0]
    nodes = out.shape[0]

    for s in range(patches):
        here = slice(grid_rows * s, grid_rows * (s + 1))
        lat[here, :] = silu(mm_tn(buf[s, :columns, :], w_embed[...])).astype(jnp.bfloat16)
    for s in range(patches):
        here = slice(grid_rows * s, grid_rows * (s + 1))
        sent[here, :] = silu(mm(lat[here, :], w_send[...])).astype(jnp.bfloat16)
    for s in range(patches):
        here = slice(grid_rows * s, grid_rows * (s + 1))
        notes = notes_of(buf, s, columns, 3 * chunks)
        to, frm = [], []
        for j in range(chunks):
            high, low = notes[chunks + j], notes[2 * chunks + j]
            key = jnp.where(high // patches == pick, (high % patches) * LANES + low, -1)
            to.append(hot_by_row(key, nodes))
            frm.append(hot_by_row(notes[j], grid_rows))
        counts[:, here] = mm_nt(side(to), side(frm)).astype(jnp.bfloat16)
    for i in range(nodes // 256):
        here = slice(256 * i, 256 * (i + 1))
        added = mm(counts[here, :], sent[...])
        out[here, :] = added if acc is None else acc[here, :] + added


def enc_first(pick, buf, w_embed, w_send, out, lat, sent, counts, *, chunks):
    band_sums(pick[0], buf, w_embed, w_send, None, out, lat, sent, counts, chunks)


def enc_more(pick, buf, w_embed, w_send, acc, out, lat, sent, counts, *, chunks):
    band_sums(pick[0], buf, w_embed, w_send, acc, out, lat, sent, counts, chunks)


def enc_last(
    pick, buf, w_embed, w_send, acc, init, gain, w_node, out, lat, sent, counts, total, *, chunks
):
    band_sums(pick[0], buf, w_embed, w_send, acc, total, lat, sent, counts, chunks)
    for i in range(out.shape[0] // 256):
        here = slice(256 * i, 256 * (i + 1))
        node_in = silu(rms(total[here, :]) * gain[...]).astype(jnp.bfloat16)
        fresh = init[here, :].astype(jnp.float32) + mm(node_in, w_node[...])
        out[here, :] = fresh.astype(jnp.bfloat16)


def picked_rows(pick, src, nodes, j):
    count = nodes.shape[0]
    hot = []
    for i in range(4 * j, 4 * j + 4):
        code = src[i : i + 1, :]
        key = jnp.where(code // count == pick, code % count, -1)
        hot.append(hot_by_column(columns_of(key), count))
    return mm(jnp.concatenate(hot, axis=0), nodes[...]).astype(jnp.bfloat16)


def proc_first(pick, src, nodes, out):
    for j in range(src.shape[0] // 4):
        out[512 * j : 512 * (j + 1), :] = picked_rows(pick[0], src, nodes, j)


def proc_more(pick, src, nodes, acc, out):
    for j in range(src.shape[0] // 4):
        at = slice(512 * j, 512 * (j + 1))
        out[at, :] = acc[at, :] + picked_rows(pick[0], src, nodes, j)


def proc_last(
    pick, src, dst, nodes, acc, band_one, w_ps, w_pr, w_po, w_ds, out, *, last_band
):
    band, mine = pick[1], out.shape[0]
    band_nodes = nodes.shape[0]
    own = band_one[pl.ds(pl.multiple_of(pick[2] * mine, mine), mine), :]
    recv = mm(own, w_pr[...])
    top = recv.astype(jnp.bfloat16)
    rest = (recv - top.astype(jnp.float32)).astype(jnp.bfloat16)
    recv_pair = jnp.concatenate([top, rest], axis=0)
    total = jnp.zeros(own.shape, jnp.float32)
    for j in range(src.shape[0] // 4):
        at = slice(512 * j, 512 * (j + 1))
        rows = acc[at, :] + picked_rows(pick[0], src, nodes, j)
        recv_hot, back = [], []
        for i in range(4 * j, 4 * j + 4):
            to = dst[i : i + 1, :]
            one = hot_by_column(columns_of(to), LANES)
            recv_hot.append(side([one, one]))
            target = band + src[i : i + 1, :] // band_nodes - 1
            valid = (target >= 0) & (target <= last_band)
            back.append(hot_by_row(jnp.where(valid, to, -1), mine))
        recv_rows = mm(jnp.concatenate(recv_hot, axis=0), recv_pair)
        msg = silu(mm(rows, w_ps[...]) + recv_rows).astype(jnp.bfloat16)
        total += mm(side(back), msg)
    norm = rms(total).astype(jnp.bfloat16)
    two = (own.astype(jnp.float32) + mm(norm, w_po[...])).astype(jnp.bfloat16)
    out[...] = silu(mm(two, w_ds[...])).astype(jnp.bfloat16)


def dec_counts(place, own, near, far, out, *, columns, skip, chunks):
    patches, _, grid_rows = own.shape
    patch, second = place[0], place[1]
    nodes = out.shape[1]
    for k, buf in enumerate((own, near, far)):
        notes = notes_of(buf, patch, columns, skip + 3 * chunks)[skip:]
        to, frm = [], []
        for j in range(chunks):
            high, low, dst = notes[j], notes[chunks + j], notes[2 * chunks + j]
            rel = (high % patches - patch) * (1 - 2 * second)
            turn = (rel + 2) & (patches - 1)
            spot = jnp.where(turn < 4, turn ^ 2, turn) ^ (3 * second)
            key = jnp.where(high // patches == place[2 + k], spot * LANES + low, -1)
            frm.append(hot_by_row(key, nodes))
            to.append(hot_by_row(dst, grid_rows))
        block = mm_nt(side(to), side(frm))
        out[grid_rows * k : grid_rows * (k + 1), :] = block.astype(jnp.bfloat16)


def dec_sums(counts, four, rest, out, *, first):
    half = four.shape[0]
    here = slice(first, first + out.shape[0])
    total = mm(counts[here, :half], four[...]) + mm(counts[here, half:], rest[...])
    out[...] = total.astype(out.dtype)


def dec_last(own, near, far, grid_vars, w_out, out):
    total = own[...] + near[...].astype(jnp.float32) + far[...].astype(jnp.float32)
    norm = rms(total).astype(jnp.bfloat16)
    fresh = grid_vars[...].astype(jnp.float32) + mm_nt(w_out[...], norm)
    out[...] = fresh.astype(jnp.bfloat16)


def call(body, out, *args, vmem=16, scalars=0, scratch=(), flops=0, **static):
    block = pl.BlockSpec(memory_space=pltpu.VMEM)
    smem = pl.BlockSpec(memory_space=pltpu.SMEM)
    moved = sum(a.size * a.dtype.itemsize for a in args) + out.size * out.dtype.itemsize
    return pl.pallas_call(
        functools.partial(body, **static),
        out_shape=out,
        in_specs=[smem] * scalars + [block] * (len(args) - scalars),
        out_specs=block,
        scratch_shapes=list(scratch),
        compiler_params=pltpu.CompilerParams(vmem_limit_bytes=vmem * MIB),
        cost_estimate=pl.CostEstimate(flops=flops, bytes_accessed=moved, transcendentals=0),
        name=body.__name__,
    )(*args)


def pair_groups(bands, patches, step):
    groups = []
    for b in range(bands):
        for p in range(patches):
            if (p + b) % 2 == 0:
                q = (p + 1) % patches if step == 0 else (p - 1) % patches
                groups.append([b * patches + p, b * patches + q])
    return groups


def shards(
    bands,
    patches,
    grid_vars,
    mesh_init,
    w_embed,
    w_send,
    w_node,
    node_gain,
    w_proc_send,
    w_proc_recv,
    w_proc_out,
    w_dec_send,
    w_dec_out,
    enc_src,
    enc_dst,
    proc_src,
    proc_dst,
    dec_src,
    dec_dst,
):
    f32, bf16 = jnp.float32, jnp.bfloat16
    shape = jax.ShapeDtypeStruct
    mine, width = mesh_init.shape
    band_nodes = patches * mine
    grid_rows, columns = grid_vars.shape
    edges = enc_src.shape[0]
    chunks = edges // LANES
    band = lax.axis_index("grid").astype(jnp.int32)
    patch = lax.axis_index("mesh").astype(jnp.int32)
    odd = band % 2
    far = 2 * odd
    near = 2 - far
    far_pairs = [(i, i + 1) for i in range(1, bands - 1, 2)]
    far_pairs += [(j, i) for i, j in far_pairs]
    near_pairs = [(i, i + 1) for i in range(0, bands - 1, 2)]
    near_pairs += [(j, i) for i, j in near_pairs]

    def over_far(block):
        return lax.ppermute(block, "grid", far_pairs)

    def over_near(block):
        return lax.ppermute(block, "grid", near_pairs)

    def scalars(*values):
        return jnp.stack(values).astype(jnp.int32)

    init_band = lax.all_gather(mesh_init, "mesh", axis=0, tiled=True)

    notes = jnp.concatenate(
        [enc_src, enc_dst // mine, enc_dst % mine, dec_src // mine, dec_src % mine, dec_dst]
    )
    note_rows = -(-(columns + -(-notes.size // grid_rows)) // 8) * 8 - columns
    notes = jnp.pad(notes, (0, note_rows * grid_rows - notes.size)).astype(bf16)
    grid_turned = grid_vars.T
    load = jnp.concatenate([grid_turned, notes.reshape(note_rows, grid_rows)], axis=0)
    own = lax.all_gather(load, "mesh", axis=0, tiled=False)
    far_load = over_far(own)
    near_load = over_near(own)

    band_rows = patches * grid_rows
    enc = dict(
        chunks=chunks,
        scalars=1,
        vmem=20,
        flops=2 * band_rows * (width * (columns + width) + band_nodes * (edges + width)),
    )
    scratch = [
        pltpu.VMEM((band_rows, width), bf16),
        pltpu.VMEM((band_rows, width), bf16),
        pltpu.VMEM((band_nodes, band_rows), bf16),
    ]
    acc_shape = shape((band_nodes, width), f32)
    acc = call(enc_first, acc_shape, scalars(1), own, w_embed, w_send, scratch=scratch, **enc)
    acc = call(
        enc_more, acc_shape, scalars(2 - near), near_load, w_embed, w_send, acc, scratch=scratch, **enc
    )
    one = call(
        enc_last,
        shape((band_nodes, width), bf16),
        scalars(2 - far),
        far_load,
        w_embed,
        w_send,
        acc,
        init_band,
        node_gain.reshape(1, width),
        w_node,
        scratch=scratch + [pltpu.VMEM((band_nodes, width), f32)],
        **enc,
    )

    far_one = over_far(one)
    near_one = over_near(one)
    src = proc_src.reshape(-1, LANES)
    dst = proc_dst.reshape(-1, LANES)
    proc_edges = proc_src.shape[0]
    pick = dict(scalars=1, flops=2 * proc_edges * band_nodes * width)
    pick_shape = shape((proc_edges, width), bf16)
    got = call(proc_first, pick_shape, scalars(1), src, one, **pick)

    second = (patch + band) % 2
    dec_edges = dec_src.shape[0]
    counts = call(
        dec_counts,
        shape((3 * grid_rows, band_nodes), bf16),
        scalars(patch, second, 1, 2 - near, 2 - far),
        own,
        near_load,
        far_load,
        scalars=1,
        flops=6 * grid_rows * band_nodes * dec_edges,
        columns=columns,
        skip=3 * chunks,
        chunks=dec_edges // LANES,
    )

    got = call(proc_more, pick_shape, scalars(near), src, near_one, got, **pick)
    sent = call(
        proc_last,
        shape((mine, width), bf16),
        scalars(far, band, patch),
        src,
        dst,
        far_one,
        got,
        one,
        w_proc_send,
        w_proc_recv,
        w_proc_out,
        w_dec_send,
        last_band=bands - 1,
        **pick,
    )

    groups = [pair_groups(bands, patches, step) for step in (0, 1)]

    def meet(rows_here, step):
        return lax.all_gather(
            rows_here, ("grid", "mesh"), axis=0, tiled=True, axis_index_groups=groups[step]
        )

    def partner_half(both):
        size = both.shape[0] // 2
        return lax.dynamic_slice_in_dim(both, (1 - second) * size, size, 0)

    four = meet(meet(sent, 0), 1)
    rest = meet(partner_half(meet(partner_half(four), 0)), 1)
    flops = 2 * grid_rows * band_nodes * width
    part = shape((grid_rows, width), bf16)
    far_sums = over_far(call(dec_sums, part, counts, four, rest, flops=flops, first=2 * grid_rows))
    near_sums = over_near(call(dec_sums, part, counts, four, rest, flops=flops, first=grid_rows))
    own_sums = call(
        dec_sums, shape((grid_rows, width), f32), counts, four, rest, flops=flops, first=0
    )
    return call(
        dec_last,
        shape((columns, grid_rows), bf16),
        own_sums,
        near_sums,
        far_sums,
        grid_turned,
        w_dec_out.T,
        flops=flops,
    ).T


def solution(mesh):
    spread = P(("grid", "mesh"), None)
    edge = P(("grid", "mesh"))
    in_specs = (spread, spread) + (P(),) * 9 + (edge,) * 6
    body = functools.partial(shards, mesh.shape["grid"], mesh.shape["mesh"])
    return jax.shard_map(body, mesh=mesh, in_specs=in_specs, out_specs=spread, check_vma=False)
```

```python
import functools

import jax
import jax.numpy as jnp
from jax import lax
from jax.experimental import pallas as pl
from jax.experimental.pallas import tpu as pltpu
from jax.sharding import PartitionSpec as P

LANES = 128
MIB = 1024 * 1024


def silu(v):
    return v * (0.5 + 0.5 * jnp.tanh(0.5 * v))


def rms(v):
    return v * lax.rsqrt(jnp.mean(v * v, axis=-1, keepdims=True) + 1e-05)


def mm(a, b):
    return jnp.dot(a, b, preferred_element_type=jnp.float32)


def mm_tn(a, b):
    return lax.dot_general(a, b, (((0,), (0,)), ((), ())), preferred_element_type=jnp.float32)


def mm_nt(a, b):
    return lax.dot_general(a, b, (((1,), (1,)), ((), ())), preferred_element_type=jnp.float32)


def hot_by_row(keys, count):
    spots = lax.broadcasted_iota(jnp.int16, (count, keys.shape[1]), 0)
    one, none = jnp.bfloat16(1), jnp.bfloat16(0)
    return jnp.where(spots == keys.astype(jnp.int16), one, none)


def columns_of(row):
    return jnp.transpose(jnp.broadcast_to(row, (LANES, LANES)))


def hot_by_column(spread, count):
    lanes = lax.broadcasted_iota(jnp.int32, (LANES, LANES), 1)
    parts = [
        jnp.where(spread == lanes + LANES * k, 1.0, 0.0).astype(jnp.bfloat16)
        for k in range(count // LANES)
    ]
    return jnp.concatenate(parts, axis=1)


def side(parts):
    return jnp.concatenate(parts, axis=1)


def notes_of(buf, s, columns, count):
    start = columns // 16 * 16
    notes = buf[s, start:, :].astype(jnp.float32).astype(jnp.int32)
    skip = columns - start

    def piece(k):
        row, lane = skip + k // 2, LANES * (k % 2)
        return notes[row : row + 1, lane : lane + LANES]

    return [piece(k) for k in range(count)]


def pack(*refs):
    out, sems = refs[5], refs[11]
    waits(fetch(sems, *zip(refs[:5], refs[6:11])))()
    grid_turned, enc_src, enc_dst, dec_src, dec_dst = refs[6:11]
    columns, grid_rows = grid_turned.shape
    start = columns // 16 * 16
    out[:start, :] = grid_turned[:start, :]
    pieces = []
    for part in (
        enc_src[...],
        enc_dst[...] // LANES,
        enc_dst[...] % LANES,
        dec_src[...] // LANES,
        dec_src[...] % LANES,
        dec_dst[...],
    ):
        part = part.astype(jnp.float32)
        pieces += [part[j : j + 1, :] for j in range(part.shape[0])]
    pieces += [jnp.zeros_like(pieces[0])] * (len(pieces) % 2)
    notes = [side(pieces[k : k + 2]) for k in range(0, len(pieces), 2)]
    blank = jnp.zeros((out.shape[0] - columns - len(notes), grid_rows), jnp.float32)
    rows = [grid_turned[start:, :].astype(jnp.float32)] + notes + [blank]
    out[start:, :] = jnp.concatenate(rows, axis=0).astype(jnp.bfloat16)


def fetch(sems, *pairs):
    copies = [pltpu.make_async_copy(a, b, sems.at[i]) for i, (a, b) in enumerate(pairs)]
    for copy in copies:
        copy.start()
    return copies


def band_sums(pick, buf, w_embed, w_send, lat, sent, counts, chunks, ready):
    patches, _, grid_rows = buf.shape
    columns = w_embed.shape[0]
    nodes = counts.shape[0]
    for s in range(patches):
        here = slice(grid_rows * s, grid_rows * (s + 1))
        notes = notes_of(buf, s, columns, 3 * chunks)
        to, frm = [], []
        for j in range(chunks):
            high, low = notes[chunks + j], notes[2 * chunks + j]
            key = jnp.where(high // patches == pick, (high % patches) * LANES + low, -1)
            to.append(hot_by_row(key, nodes))
            frm.append(hot_by_row(notes[j], grid_rows))
        counts[:, here] = mm_nt(side(to), side(frm)).astype(jnp.bfloat16)
    ready()
    for s in range(patches):
        here = slice(grid_rows * s, grid_rows * (s + 1))
        lat[here, :] = silu(mm_tn(buf[s, :columns, :], w_embed[...])).astype(jnp.bfloat16)
    for s in range(patches):
        here = slice(grid_rows * s, grid_rows * (s + 1))
        sent[here, :] = silu(mm(lat[here, :], w_send[...])).astype(jnp.bfloat16)


def waits(copies):
    def ready():
        for copy in copies:
            copy.wait()

    return ready


def blocks(count):
    return [slice(i, i + 256) for i in range(0, count, 256)]


def enc_first(pick, buf, w_embed, w_send, out, lat, sent, counts, embed, send, sems, *, chunks):
    copies = fetch(sems, (w_embed, embed), (w_send, send))
    band_sums(pick[0], buf, embed, send, lat, sent, counts, chunks, waits(copies))
    for here in blocks(out.shape[0]):
        out[here, :] = mm(counts[here, :], sent[...])


def enc_more(
    pick, buf, acc, w_embed, w_send, out, lat, sent, counts, embed, send, sems, total, *, chunks
):
    copies = fetch(sems, (w_embed, embed), (w_send, send))
    band_sums(pick[0], buf, embed, send, lat, sent, counts, chunks, waits(copies))
    leaving = []
    for i, here in enumerate(blocks(out.shape[0])):
        total[here, :] = acc[here, :] + mm(counts[here, :], sent[...])
        copy = pltpu.make_async_copy(total.at[here, :], out.at[here, :], sems.at[2 + i])
        copy.start()
        leaving.append(copy)
    waits(leaving)()


def enc_last(
    pick,
    buf,
    gain,
    w_embed,
    w_send,
    acc,
    init,
    w_node,
    out,
    lat,
    sent,
    counts,
    embed,
    send,
    sems,
    total,
    init_here,
    node,
    *,
    chunks,
):
    copies = fetch(
        sems, (w_embed, embed), (w_send, send), (acc, total), (w_node, node), (init, init_here)
    )
    band_sums(pick[0], buf, embed, send, lat, sent, counts, chunks, waits(copies))
    for here in blocks(out.shape[0]):
        summed = total[here, :] + mm(counts[here, :], sent[...])
        node_in = silu(rms(summed) * gain[...]).astype(jnp.bfloat16)
        fresh = init_here[here, :].astype(jnp.float32) + mm(node_in, node[...])
        out[here, :] = fresh.astype(jnp.bfloat16)


def picked_rows(pick, src, nodes, j):
    count = nodes.shape[0]
    hot = []
    for i in range(4 * j, 4 * j + 4):
        code = src[i : i + 1, :]
        key = jnp.where(code // count == pick, code % count, -1)
        hot.append(hot_by_column(columns_of(key), count))
    return mm(jnp.concatenate(hot, axis=0), nodes[...]).astype(jnp.bfloat16)


def proc_first(pick, src, nodes, out):
    for j in range(src.shape[0] // 4):
        out[512 * j : 512 * (j + 1), :] = picked_rows(pick[0], src, nodes, j)


def proc_more(pick, src, nodes, acc, out):
    for j in range(src.shape[0] // 4):
        at = slice(512 * j, 512 * (j + 1))
        out[at, :] = acc[at, :] + picked_rows(pick[0], src, nodes, j)


def proc_last(
    pick, src, dst, nodes, acc, band_one, w_ps, w_pr, w_po, w_ds, out, *, last_band
):
    band, mine = pick[1], out.shape[0]
    band_nodes = nodes.shape[0]
    own = band_one[pl.ds(pl.multiple_of(pick[2] * mine, mine), mine), :]
    recv = mm(own, w_pr[...])
    top = recv.astype(jnp.bfloat16)
    rest = (recv - top.astype(jnp.float32)).astype(jnp.bfloat16)
    recv_pair = jnp.concatenate([top, rest], axis=0)
    total = jnp.zeros(own.shape, jnp.float32)
    for j in range(src.shape[0] // 4):
        at = slice(512 * j, 512 * (j + 1))
        rows = acc[at, :] + picked_rows(pick[0], src, nodes, j)
        recv_hot, back = [], []
        for i in range(4 * j, 4 * j + 4):
            to = dst[i : i + 1, :]
            one = hot_by_column(columns_of(to), LANES)
            recv_hot.append(side([one, one]))
            target = band + src[i : i + 1, :] // band_nodes - 1
            valid = (target >= 0) & (target <= last_band)
            back.append(hot_by_row(jnp.where(valid, to, -1), mine))
        recv_rows = mm(jnp.concatenate(recv_hot, axis=0), recv_pair)
        msg = silu(mm(rows, w_ps[...]) + recv_rows).astype(jnp.bfloat16)
        total += mm(side(back), msg)
    norm = rms(total).astype(jnp.bfloat16)
    two = (own.astype(jnp.float32) + mm(norm, w_po[...])).astype(jnp.bfloat16)
    out[...] = silu(mm(two, w_ds[...])).astype(jnp.bfloat16)


def dec_counts(place, own, near, far, out, *, columns, skip, chunks):
    patches, _, grid_rows = own.shape
    patch, second = place[0], place[1]
    nodes = out.shape[1]
    for k, buf in enumerate((own, near, far)):
        notes = notes_of(buf, patch, columns, skip + 3 * chunks)[skip:]
        to, frm = [], []
        for j in range(chunks):
            high, low, dst = notes[j], notes[chunks + j], notes[2 * chunks + j]
            rel = (high % patches - patch) * (1 - 2 * second)
            turn = (rel + 2) & (patches - 1)
            spot = jnp.where(turn < 4, turn ^ 2, turn) ^ (3 * second)
            key = jnp.where(high // patches == place[2 + k], spot * LANES + low, -1)
            frm.append(hot_by_row(key, nodes))
            to.append(hot_by_row(dst, grid_rows))
        block = mm_nt(side(to), side(frm))
        out[grid_rows * k : grid_rows * (k + 1), :] = block.astype(jnp.bfloat16)


def dec_sums(counts, four, rest, out, *, first):
    half = four.shape[0]
    here = slice(first, first + out.shape[0])
    total = mm(counts[here, :half], four[...]) + mm(counts[here, half:], rest[...])
    out[...] = total.astype(out.dtype)


def dec_last(own, near, far, grid_vars, w_out, out):
    total = own[...] + near[...].astype(jnp.float32) + far[...].astype(jnp.float32)
    norm = rms(total).astype(jnp.bfloat16)
    fresh = grid_vars[...].astype(jnp.float32) + mm_nt(w_out[...], norm)
    out[...] = fresh.astype(jnp.bfloat16)


def call(body, out, *args, vmem=16, scalars=0, remote=0, out_remote=False, scratch=(), flops=0, **static):
    block = pl.BlockSpec(memory_space=pltpu.VMEM)
    smem = pl.BlockSpec(memory_space=pltpu.SMEM)
    away = pl.BlockSpec(memory_space=pltpu.HBM)
    args = list(args)
    args[len(args) - remote :] = [
        pltpu.with_memory_space_constraint(a, pltpu.HBM) for a in args[len(args) - remote :]
    ]
    moved = sum(a.size * a.dtype.itemsize for a in args) + out.size * out.dtype.itemsize
    return pl.pallas_call(
        functools.partial(body, **static),
        out_shape=pltpu.HBM(out.shape, out.dtype) if out_remote else out,
        in_specs=[smem] * scalars + [block] * (len(args) - scalars - remote) + [away] * remote,
        out_specs=away if out_remote else block,
        scratch_shapes=list(scratch),
        compiler_params=pltpu.CompilerParams(vmem_limit_bytes=vmem * MIB),
        cost_estimate=pl.CostEstimate(flops=flops, bytes_accessed=moved, transcendentals=0),
        name=body.__name__,
    )(*args)


def pair_groups(bands, patches, step):
    groups = []
    for b in range(bands):
        for p in range(patches):
            if (p + b) % 2 == 0:
                q = (p + 1) % patches if step == 0 else (p - 1) % patches
                groups.append([b * patches + p, b * patches + q])
    return groups


def shards(
    bands,
    patches,
    grid_vars,
    mesh_init,
    w_embed,
    w_send,
    w_node,
    node_gain,
    w_proc_send,
    w_proc_recv,
    w_proc_out,
    w_dec_send,
    w_dec_out,
    enc_src,
    enc_dst,
    proc_src,
    proc_dst,
    dec_src,
    dec_dst,
):
    f32, bf16 = jnp.float32, jnp.bfloat16
    shape = jax.ShapeDtypeStruct
    mine, width = mesh_init.shape
    band_nodes = patches * mine
    grid_rows, columns = grid_vars.shape
    edges = enc_src.shape[0]
    chunks = edges // LANES
    band = lax.axis_index("grid").astype(jnp.int32)
    patch = lax.axis_index("mesh").astype(jnp.int32)
    odd = band % 2
    far = 2 * odd
    near = 2 - far
    far_pairs = [(i, i + 1) for i in range(1, bands - 1, 2)]
    far_pairs += [(j, i) for i, j in far_pairs]
    near_pairs = [(i, i + 1) for i in range(0, bands - 1, 2)]
    near_pairs += [(j, i) for i, j in near_pairs]

    def over_far(block):
        return lax.ppermute(block, "grid", far_pairs)

    def over_near(block):
        return lax.ppermute(block, "grid", near_pairs)

    def scalars(*values):
        return jnp.stack(values).astype(jnp.int32)

    init_band = lax.all_gather(mesh_init, "mesh", axis=0, tiled=True)

    note_count = -(-(3 * edges + 3 * dec_src.size) // grid_rows)
    load_rows = -(-(columns + note_count) // 8) * 8
    grid_turned = grid_vars.T
    parts = [grid_turned]
    parts += [a.reshape(-1, LANES) for a in (enc_src, enc_dst, dec_src, dec_dst)]
    load = call(
        pack,
        shape((load_rows, grid_rows), bf16),
        *parts,
        remote=5,
        scratch=[pltpu.VMEM(a.shape, a.dtype) for a in parts] + [pltpu.SemaphoreType.DMA((5,))],
    )
    own = lax.all_gather(load, "mesh", axis=0, tiled=False)
    far_load = over_far(own)
    near_load = over_near(own)

    band_rows = patches * grid_rows
    enc = dict(
        chunks=chunks,
        scalars=1,
        vmem=20,
        flops=2 * band_rows * (width * (columns + width) + band_nodes * (edges + width)),
    )
    scratch = [
        pltpu.VMEM((band_rows, width), bf16),
        pltpu.VMEM((band_rows, width), bf16),
        pltpu.VMEM((band_nodes, band_rows), bf16),
        pltpu.VMEM((columns, width), bf16),
        pltpu.VMEM((width, width), bf16),
        pltpu.SemaphoreType.DMA((6,)),
    ]
    held = pltpu.VMEM((band_nodes, width), f32)
    acc_shape = shape((band_nodes, width), f32)
    acc = call(
        enc_first, acc_shape, scalars(1), own, w_embed, w_send, remote=2, scratch=scratch, **enc
    )
    acc = call(
        enc_more,
        acc_shape,
        scalars(2 - near),
        near_load,
        acc,
        w_embed,
        w_send,
        remote=2,
        out_remote=True,
        scratch=scratch + [held],
        **enc,
    )
    one = call(
        enc_last,
        shape((band_nodes, width), bf16),
        scalars(2 - far),
        far_load,
        node_gain.reshape(1, width),
        w_embed,
        w_send,
        acc,
        init_band,
        w_node,
        remote=5,
        scratch=scratch
        + [held, pltpu.VMEM((band_nodes, width), bf16), pltpu.VMEM((width, width), bf16)],
        **enc,
    )

    far_one = over_far(one)
    near_one = over_near(one)
    src = proc_src.reshape(-1, LANES)
    dst = proc_dst.reshape(-1, LANES)
    proc_edges = proc_src.shape[0]
    pick = dict(scalars=1, flops=2 * proc_edges * band_nodes * width)
    pick_shape = shape((proc_edges, width), bf16)
    got = call(proc_first, pick_shape, scalars(1), src, one, **pick)

    second = (patch + band) % 2
    dec_edges = dec_src.shape[0]
    counts = call(
        dec_counts,
        shape((3 * grid_rows, band_nodes), bf16),
        scalars(patch, second, 1, 2 - near, 2 - far),
        own,
        near_load,
        far_load,
        scalars=1,
        flops=6 * grid_rows * band_nodes * dec_edges,
        columns=columns,
        skip=3 * chunks,
        chunks=dec_edges // LANES,
    )

    got = call(proc_more, pick_shape, scalars(near), src, near_one, got, **pick)
    sent = call(
        proc_last,
        shape((mine, width), bf16),
        scalars(far, band, patch),
        src,
        dst,
        far_one,
        got,
        one,
        w_proc_send,
        w_proc_recv,
        w_proc_out,
        w_dec_send,
        last_band=bands - 1,
        **pick,
    )

    groups = [pair_groups(bands, patches, step) for step in (0, 1)]

    def meet(rows_here, step):
        return lax.all_gather(
            rows_here, ("grid", "mesh"), axis=0, tiled=True, axis_index_groups=groups[step]
        )

    def partner_half(both):
        size = both.shape[0] // 2
        return lax.dynamic_slice_in_dim(both, (1 - second) * size, size, 0)

    four = meet(meet(sent, 0), 1)
    rest = meet(partner_half(meet(partner_half(four), 0)), 1)
    flops = 2 * grid_rows * band_nodes * width
    part = shape((grid_rows, width), bf16)
    far_sums = over_far(call(dec_sums, part, counts, four, rest, flops=flops, first=2 * grid_rows))
    near_sums = over_near(call(dec_sums, part, counts, four, rest, flops=flops, first=grid_rows))
    own_sums = call(
        dec_sums, shape((grid_rows, width), f32), counts, four, rest, flops=flops, first=0
    )
    return call(
        dec_last,
        shape((columns, grid_rows), bf16),
        own_sums,
        near_sums,
        far_sums,
        grid_turned,
        w_dec_out.T,
        flops=flops,
    ).T


def solution(mesh):
    spread = P(("grid", "mesh"), None)
    edge = P(("grid", "mesh"))
    in_specs = (spread, spread) + (P(),) * 9 + (edge,) * 6
    body = functools.partial(shards, mesh.shape["grid"], mesh.shape["mesh"])
    return jax.shard_map(body, mesh=mesh, in_specs=in_specs, out_specs=spread, check_vma=False)
```

```python
import functools

import jax
import jax.numpy as jnp
from jax import lax
from jax.experimental import pallas as pl
from jax.experimental.pallas import tpu as pltpu
from jax.sharding import PartitionSpec as P

LANES = 128
MIB = 1024 * 1024


def silu(v):
    return v * (0.5 + 0.5 * jnp.tanh(0.5 * v))


def rms(v):
    return v * lax.rsqrt(jnp.mean(v * v, axis=-1, keepdims=True) + 1e-05)


def mm(a, b):
    return jnp.dot(a, b, preferred_element_type=jnp.float32)


def mm_tn(a, b):
    return lax.dot_general(a, b, (((0,), (0,)), ((), ())), preferred_element_type=jnp.float32)


def mm_nt(a, b):
    return lax.dot_general(a, b, (((1,), (1,)), ((), ())), preferred_element_type=jnp.float32)


def hot_by_row(keys, count):
    spots = lax.broadcasted_iota(jnp.int16, (count, keys.shape[1]), 0)
    one, none = jnp.bfloat16(1), jnp.bfloat16(0)
    return jnp.where(spots == keys.astype(jnp.int16), one, none)


def marks(rows, count):
    return side([hot_by_row(row, count).astype(jnp.float8_e4m3fn) for row in rows])


def columns_of(row):
    return jnp.transpose(jnp.broadcast_to(row, (LANES, LANES)))


def hot_by_column(spread, count):
    lanes = lax.broadcasted_iota(jnp.int32, (LANES, LANES), 1)
    parts = [
        jnp.where(spread == lanes + LANES * k, 1.0, 0.0).astype(jnp.bfloat16)
        for k in range(count // LANES)
    ]
    return jnp.concatenate(parts, axis=1)


def side(parts):
    return jnp.concatenate(parts, axis=1)


def notes_of(buf, s, columns, count):
    start = columns // 16 * 16
    notes = buf[s, start:, :].astype(jnp.float32).astype(jnp.int32)
    skip = columns - start

    def piece(k):
        row, lane = skip + k // 2, LANES * (k % 2)
        return notes[row : row + 1, lane : lane + LANES]

    return [piece(k) for k in range(count)]


def pack(*refs):
    out, sems = refs[5], refs[11]
    waits(fetch(sems, *zip(refs[:5], refs[6:11])))()
    grid_turned, enc_src, enc_dst, dec_src, dec_dst = refs[6:11]
    columns, grid_rows = grid_turned.shape
    start = columns // 16 * 16
    out[:start, :] = grid_turned[:start, :]
    pieces = []
    for part in (
        enc_src[...],
        enc_dst[...] // LANES,
        enc_dst[...] % LANES,
        dec_src[...] // LANES,
        dec_src[...] % LANES,
        dec_dst[...],
    ):
        part = part.astype(jnp.float32)
        pieces += [part[j : j + 1, :] for j in range(part.shape[0])]
    pieces += [jnp.zeros_like(pieces[0])] * (len(pieces) % 2)
    notes = [side(pieces[k : k + 2]) for k in range(0, len(pieces), 2)]
    blank = jnp.zeros((out.shape[0] - columns - len(notes), grid_rows), jnp.float32)
    rows = [grid_turned[start:, :].astype(jnp.float32)] + notes + [blank]
    out[start:, :] = jnp.concatenate(rows, axis=0).astype(jnp.bfloat16)


def fetch(sems, *pairs):
    copies = [pltpu.make_async_copy(a, b, sems.at[i]) for i, (a, b) in enumerate(pairs)]
    for copy in copies:
        copy.start()
    return copies


def band_sums(pick, buf, w_embed, w_send, lat, sent, counts, chunks, ready):
    patches, _, grid_rows = buf.shape
    columns = w_embed.shape[0]
    nodes = counts.shape[0]
    for s in range(patches):
        here = slice(grid_rows * s, grid_rows * (s + 1))
        notes = notes_of(buf, s, columns, 3 * chunks)
        to, frm = [], []
        for j in range(chunks):
            high, low = notes[chunks + j], notes[2 * chunks + j]
            key = jnp.where(high // patches == pick, (high % patches) * LANES + low, -1)
            to.append(key)
            frm.append(notes[j])
        counts[:, here] = mm_nt(marks(to, nodes), marks(frm, grid_rows)).astype(jnp.bfloat16)
    ready()
    for s in range(patches):
        here = slice(grid_rows * s, grid_rows * (s + 1))
        lat[here, :] = silu(mm_tn(buf[s, :columns, :], w_embed[...])).astype(jnp.bfloat16)
    for s in range(patches):
        here = slice(grid_rows * s, grid_rows * (s + 1))
        sent[here, :] = silu(mm(lat[here, :], w_send[...])).astype(jnp.bfloat16)


def waits(copies):
    def ready():
        for copy in copies:
            copy.wait()

    return ready


def blocks(count):
    return [slice(i, i + 256) for i in range(0, count, 256)]


def enc_first(pick, buf, w_embed, w_send, out, lat, sent, counts, embed, send, sems, *, chunks):
    copies = fetch(sems, (w_embed, embed), (w_send, send))
    band_sums(pick[0], buf, embed, send, lat, sent, counts, chunks, waits(copies))
    for here in blocks(out.shape[0]):
        out[here, :] = mm(counts[here, :], sent[...])


def enc_more(
    pick, buf, acc, w_embed, w_send, out, lat, sent, counts, embed, send, sems, *, chunks
):
    copies = fetch(sems, (w_embed, embed), (w_send, send))
    band_sums(pick[0], buf, embed, send, lat, sent, counts, chunks, waits(copies))
    for here in blocks(out.shape[0]):
        out[here, :] = acc[here, :] + mm(counts[here, :], sent[...])


def enc_last(
    pick, buf, acc, gain, w_embed, w_send, out, lat, sent, counts, embed, send, sems, *, chunks
):
    copies = fetch(sems, (w_embed, embed), (w_send, send))
    band_sums(pick[0], buf, embed, send, lat, sent, counts, chunks, waits(copies))
    for here in blocks(out.shape[0]):
        summed = acc[here, :] + mm(counts[here, :], sent[...])
        out[here, :] = silu(rms(summed) * gain[...]).astype(jnp.bfloat16)


def node_update(node_in, w_node, init, out, node, init_here, sems):
    parts = blocks(out.shape[0])
    copies = fetch(
        sems, (w_node, node), *[(init.at[here, :], init_here.at[here, :]) for here in parts]
    )
    copies[0].wait()
    for i, here in enumerate(parts):
        fresh = mm(node_in[here, :], node[...])
        copies[1 + i].wait()
        out[here, :] = (init_here[here, :].astype(jnp.float32) + fresh).astype(jnp.bfloat16)


def picked_rows(pick, src, nodes, j):
    count = nodes.shape[0]
    hot = []
    for i in range(4 * j, 4 * j + 4):
        code = src[i : i + 1, :]
        key = jnp.where(code // count == pick, code % count, -1)
        hot.append(hot_by_column(columns_of(key), count))
    return mm(jnp.concatenate(hot, axis=0), nodes[...]).astype(jnp.bfloat16)


def proc_first(pick, src, nodes, out):
    for j in range(src.shape[0] // 4):
        out[512 * j : 512 * (j + 1), :] = picked_rows(pick[0], src, nodes, j)


def proc_more(pick, src, nodes, acc, out):
    for j in range(src.shape[0] // 4):
        at = slice(512 * j, 512 * (j + 1))
        out[at, :] = acc[at, :] + picked_rows(pick[0], src, nodes, j)


def proc_last(
    pick, src, dst, nodes, acc, band_one, w_ps, w_pr, w_po, w_ds, out, *, last_band
):
    band, mine = pick[1], out.shape[0]
    band_nodes = nodes.shape[0]
    own = band_one[pl.ds(pl.multiple_of(pick[2] * mine, mine), mine), :]
    recv = mm(own, w_pr[...])
    top = recv.astype(jnp.bfloat16)
    rest = (recv - top.astype(jnp.float32)).astype(jnp.bfloat16)
    recv_pair = jnp.concatenate([top, rest], axis=0)
    total = jnp.zeros(own.shape, jnp.float32)
    for j in range(src.shape[0] // 4):
        at = slice(512 * j, 512 * (j + 1))
        rows = acc[at, :] + picked_rows(pick[0], src, nodes, j)
        recv_hot, back = [], []
        for i in range(4 * j, 4 * j + 4):
            to = dst[i : i + 1, :]
            one = hot_by_column(columns_of(to), LANES)
            recv_hot.append(side([one, one]))
            target = band + src[i : i + 1, :] // band_nodes - 1
            valid = (target >= 0) & (target <= last_band)
            back.append(hot_by_row(jnp.where(valid, to, -1), mine))
        recv_rows = mm(jnp.concatenate(recv_hot, axis=0), recv_pair)
        msg = silu(mm(rows, w_ps[...]) + recv_rows).astype(jnp.bfloat16)
        total += mm(side(back), msg)
    norm = rms(total).astype(jnp.bfloat16)
    two = (own.astype(jnp.float32) + mm(norm, w_po[...])).astype(jnp.bfloat16)
    out[...] = silu(mm(two, w_ds[...])).astype(jnp.bfloat16)


def dec_counts(place, own, near, far, out, *, columns, skip, chunks):
    patches, _, grid_rows = own.shape
    patch, second = place[0], place[1]
    nodes = out.shape[1]
    for k, buf in enumerate((own, near, far)):
        notes = notes_of(buf, patch, columns, skip + 3 * chunks)[skip:]
        to, frm = [], []
        for j in range(chunks):
            high, low, dst = notes[j], notes[chunks + j], notes[2 * chunks + j]
            rel = (high % patches - patch) * (1 - 2 * second)
            turn = (rel + 2) & (patches - 1)
            spot = jnp.where(turn < 4, turn ^ 2, turn) ^ (3 * second)
            key = jnp.where(high // patches == place[2 + k], spot * LANES + low, -1)
            frm.append(key)
            to.append(dst)
        block = mm_nt(marks(to, grid_rows), marks(frm, nodes))
        out[grid_rows * k : grid_rows * (k + 1), :] = block.astype(jnp.bfloat16)


def dec_sums(counts, four, rest, out, *, first):
    half = four.shape[0]
    here = slice(first, first + out.shape[0])
    total = mm(counts[here, :half], four[...]) + mm(counts[here, half:], rest[...])
    out[...] = total.astype(out.dtype)


def dec_last(own, near, far, grid_vars, w_out, out):
    total = own[...] + near[...].astype(jnp.float32) + far[...].astype(jnp.float32)
    norm = rms(total).astype(jnp.bfloat16)
    fresh = grid_vars[...].astype(jnp.float32) + mm_nt(w_out[...], norm)
    out[...] = fresh.astype(jnp.bfloat16)


def call(body, out, *args, vmem=16, scalars=0, remote=0, scratch=(), flops=0, **static):
    block = pl.BlockSpec(memory_space=pltpu.VMEM)
    smem = pl.BlockSpec(memory_space=pltpu.SMEM)
    away = pl.BlockSpec(memory_space=pltpu.HBM)
    args = list(args)
    args[len(args) - remote :] = [
        pltpu.with_memory_space_constraint(a, pltpu.HBM) for a in args[len(args) - remote :]
    ]
    moved = sum(a.size * a.dtype.itemsize for a in args) + out.size * out.dtype.itemsize
    return pl.pallas_call(
        functools.partial(body, **static),
        out_shape=out,
        in_specs=[smem] * scalars + [block] * (len(args) - scalars - remote) + [away] * remote,
        out_specs=block,
        scratch_shapes=list(scratch),
        compiler_params=pltpu.CompilerParams(vmem_limit_bytes=vmem * MIB),
        cost_estimate=pl.CostEstimate(flops=flops, bytes_accessed=moved, transcendentals=0),
        name=body.__name__,
    )(*args)


def pair_groups(bands, patches, step):
    groups = []
    for b in range(bands):
        for p in range(patches):
            if (p + b) % 2 == 0:
                q = (p + 1) % patches if step == 0 else (p - 1) % patches
                groups.append([b * patches + p, b * patches + q])
    return groups


def shards(
    bands,
    patches,
    grid_vars,
    mesh_init,
    w_embed,
    w_send,
    w_node,
    node_gain,
    w_proc_send,
    w_proc_recv,
    w_proc_out,
    w_dec_send,
    w_dec_out,
    enc_src,
    enc_dst,
    proc_src,
    proc_dst,
    dec_src,
    dec_dst,
):
    f32, bf16 = jnp.float32, jnp.bfloat16
    shape = jax.ShapeDtypeStruct
    mine, width = mesh_init.shape
    band_nodes = patches * mine
    grid_rows, columns = grid_vars.shape
    edges = enc_src.shape[0]
    chunks = edges // LANES
    band = lax.axis_index("grid").astype(jnp.int32)
    patch = lax.axis_index("mesh").astype(jnp.int32)
    odd = band % 2
    far = 2 * odd
    near = 2 - far
    far_pairs = [(i, i + 1) for i in range(1, bands - 1, 2)]
    far_pairs += [(j, i) for i, j in far_pairs]
    near_pairs = [(i, i + 1) for i in range(0, bands - 1, 2)]
    near_pairs += [(j, i) for i, j in near_pairs]

    def over_far(block):
        return lax.ppermute(block, "grid", far_pairs)

    def over_near(block):
        return lax.ppermute(block, "grid", near_pairs)

    def scalars(*values):
        return jnp.stack(values).astype(jnp.int32)

    init_band = lax.all_gather(mesh_init, "mesh", axis=0, tiled=True)

    note_count = -(-(3 * edges + 3 * dec_src.size) // grid_rows)
    load_rows = -(-(columns + note_count) // 8) * 8
    grid_turned = grid_vars.T
    parts = [grid_turned]
    parts += [a.reshape(-1, LANES) for a in (enc_src, enc_dst, dec_src, dec_dst)]
    load = call(
        pack,
        shape((load_rows, grid_rows), bf16),
        *parts,
        remote=5,
        scratch=[pltpu.VMEM(a.shape, a.dtype) for a in parts] + [pltpu.SemaphoreType.DMA((5,))],
    )
    own = lax.all_gather(load, "mesh", axis=0, tiled=False)
    far_load = over_far(own)
    near_load = over_near(own)

    band_rows = patches * grid_rows
    enc = dict(
        chunks=chunks,
        scalars=1,
        vmem=20,
        flops=band_rows * width,
    )
    scratch = [
        pltpu.VMEM((band_rows, width), bf16),
        pltpu.VMEM((band_rows, width), bf16),
        pltpu.VMEM((band_nodes, band_rows), bf16),
        pltpu.VMEM((columns, width), bf16),
        pltpu.VMEM((width, width), bf16),
        pltpu.SemaphoreType.DMA((2,)),
    ]
    acc_shape = shape((band_nodes, width), f32)
    acc = call(
        enc_first, acc_shape, scalars(1), own, w_embed, w_send, remote=2, scratch=scratch, **enc
    )
    acc = call(
        enc_more,
        acc_shape,
        scalars(2 - near),
        near_load,
        acc,
        w_embed,
        w_send,
        remote=2,
        scratch=scratch,
        **enc,
    )
    one_shape = shape((band_nodes, width), bf16)
    node_in = call(
        enc_last,
        one_shape,
        scalars(2 - far),
        far_load,
        acc,
        node_gain.reshape(1, width),
        w_embed,
        w_send,
        remote=2,
        scratch=scratch,
        **enc,
    )
    one = call(
        node_update,
        one_shape,
        node_in,
        w_node,
        init_band,
        remote=2,
        scratch=[
            pltpu.VMEM((width, width), bf16),
            pltpu.VMEM((band_nodes, width), bf16),
            pltpu.SemaphoreType.DMA((1 + band_nodes // 256,)),
        ],
    )

    far_one = over_far(one)
    near_one = over_near(one)
    src = proc_src.reshape(-1, LANES)
    dst = proc_dst.reshape(-1, LANES)
    proc_edges = proc_src.shape[0]
    pick = dict(scalars=1, flops=2 * proc_edges * band_nodes * width)
    pick_shape = shape((proc_edges, width), bf16)
    got = call(proc_first, pick_shape, scalars(1), src, one, **pick)

    second = (patch + band) % 2
    dec_edges = dec_src.shape[0]
    counts = call(
        dec_counts,
        shape((3 * grid_rows, band_nodes), bf16),
        scalars(patch, second, 1, 2 - near, 2 - far),
        own,
        near_load,
        far_load,
        scalars=1,
        flops=6 * grid_rows * band_nodes * dec_edges,
        columns=columns,
        skip=3 * chunks,
        chunks=dec_edges // LANES,
    )

    got = call(proc_more, pick_shape, scalars(near), src, near_one, got, **pick)
    sent = call(
        proc_last,
        shape((mine, width), bf16),
        scalars(far, band, patch),
        src,
        dst,
        far_one,
        got,
        one,
        w_proc_send,
        w_proc_recv,
        w_proc_out,
        w_dec_send,
        last_band=bands - 1,
        **pick,
    )

    groups = [pair_groups(bands, patches, step) for step in (0, 1)]

    def meet(rows_here, step):
        return lax.all_gather(
            rows_here, ("grid", "mesh"), axis=0, tiled=True, axis_index_groups=groups[step]
        )

    def partner_half(both):
        size = both.shape[0] // 2
        return lax.dynamic_slice_in_dim(both, (1 - second) * size, size, 0)

    four = meet(meet(sent, 0), 1)
    rest = meet(partner_half(meet(partner_half(four), 0)), 1)
    flops = 2 * grid_rows * band_nodes * width
    part = shape((grid_rows, width), bf16)
    far_sums = over_far(call(dec_sums, part, counts, four, rest, flops=flops, first=2 * grid_rows))
    near_sums = over_near(call(dec_sums, part, counts, four, rest, flops=flops, first=grid_rows))
    own_sums = call(
        dec_sums, shape((grid_rows, width), f32), counts, four, rest, flops=flops, first=0
    )
    return call(
        dec_last,
        shape((columns, grid_rows), bf16),
        own_sums,
        near_sums,
        far_sums,
        grid_turned,
        w_dec_out.T,
        flops=flops,
    ).T


def solution(mesh):
    spread = P(("grid", "mesh"), None)
    edge = P(("grid", "mesh"))
    in_specs = (spread, spread) + (P(),) * 9 + (edge,) * 6
    body = functools.partial(shards, mesh.shape["grid"], mesh.shape["mesh"])
    return jax.shard_map(body, mesh=mesh, in_specs=in_specs, out_specs=spread, check_vma=False)
```

```python
import functools

import jax
import jax.numpy as jnp
from jax import lax
from jax.experimental import pallas as pl
from jax.experimental.pallas import tpu as pltpu
from jax.sharding import PartitionSpec as P

LANES = 128
MIB = 1024 * 1024


def silu(v):
    return v * (0.5 + 0.5 * jnp.tanh(0.5 * v))


def rms(v):
    return v * lax.rsqrt(jnp.mean(v * v, axis=-1, keepdims=True) + 1e-05)


def mm(a, b):
    return jnp.dot(a, b, preferred_element_type=jnp.float32)


def mm_tn(a, b):
    return lax.dot_general(a, b, (((0,), (0,)), ((), ())), preferred_element_type=jnp.float32)


def mm_nt(a, b):
    return lax.dot_general(a, b, (((1,), (1,)), ((), ())), preferred_element_type=jnp.float32)


def hot_by_row(keys, count):
    spots = lax.broadcasted_iota(jnp.int16, (count, keys.shape[1]), 0)
    one, none = jnp.bfloat16(1), jnp.bfloat16(0)
    return jnp.where(spots == keys.astype(jnp.int16), one, none)


def marks(rows, count):
    return side([hot_by_row(row, count).astype(jnp.float8_e4m3fn) for row in rows])


def columns_of(row):
    return jnp.transpose(jnp.broadcast_to(row, (LANES, LANES)))


def hot_by_column(spread, count):
    lanes = lax.broadcasted_iota(jnp.int32, (LANES, LANES), 1)
    parts = [
        jnp.where(spread == lanes + LANES * k, 1.0, 0.0).astype(jnp.bfloat16)
        for k in range(count // LANES)
    ]
    return jnp.concatenate(parts, axis=1)


def side(parts):
    return jnp.concatenate(parts, axis=1)


def notes_of(buf, s, columns, count):
    start = columns // 16 * 16
    notes = buf[s, start:, :].astype(jnp.float32).astype(jnp.int32)
    skip = columns - start

    def piece(k):
        row, lane = skip + k // 2, LANES * (k % 2)
        return notes[row : row + 1, lane : lane + LANES]

    return [piece(k) for k in range(count)]


def pack(*refs):
    out, sems = refs[5], refs[11]
    waits(fetch(sems, *zip(refs[:5], refs[6:11])))()
    grid_turned, enc_src, enc_dst, dec_src, dec_dst = refs[6:11]
    columns, grid_rows = grid_turned.shape
    start = columns // 16 * 16
    out[:start, :] = grid_turned[:start, :]
    pieces = []
    for part in (
        enc_src[...],
        enc_dst[...] // LANES,
        enc_dst[...] % LANES,
        dec_src[...] // LANES,
        dec_src[...] % LANES,
        dec_dst[...],
    ):
        part = part.astype(jnp.float32)
        pieces += [part[j : j + 1, :] for j in range(part.shape[0])]
    pieces += [jnp.zeros_like(pieces[0])] * (len(pieces) % 2)
    notes = [side(pieces[k : k + 2]) for k in range(0, len(pieces), 2)]
    blank = jnp.zeros((out.shape[0] - columns - len(notes), grid_rows), jnp.float32)
    rows = [grid_turned[start:, :].astype(jnp.float32)] + notes + [blank]
    out[start:, :] = jnp.concatenate(rows, axis=0).astype(jnp.bfloat16)


def fetch(sems, *pairs):
    copies = [pltpu.make_async_copy(a, b, sems.at[i]) for i, (a, b) in enumerate(pairs)]
    for copy in copies:
        copy.start()
    return copies


def band_sums(pick, buf, w_embed, w_send, lat, sent, counts, chunks, ready):
    patches, _, grid_rows = buf.shape
    columns = w_embed.shape[0]
    nodes = counts.shape[0]
    across = nodes // LANES
    for s in range(patches):
        here = slice(grid_rows * s, grid_rows * (s + 1))
        notes = notes_of(buf, s, columns, 3 * chunks)
        to, frm = [], []
        for j in range(chunks):
            high, low = notes[chunks + j], notes[2 * chunks + j]
            key = jnp.where(high // across == pick, (high % across) * LANES + low, -1)
            to.append(key)
            frm.append(notes[j])
        counts[:, here] = mm_nt(marks(to, nodes), marks(frm, grid_rows)).astype(jnp.bfloat16)
    ready()
    for s in range(patches):
        here = slice(grid_rows * s, grid_rows * (s + 1))
        lat[here, :] = silu(mm_tn(buf[s, :columns, :], w_embed[...])).astype(jnp.bfloat16)
    for s in range(patches):
        here = slice(grid_rows * s, grid_rows * (s + 1))
        sent[here, :] = silu(mm(lat[here, :], w_send[...])).astype(jnp.bfloat16)


def waits(copies):
    def ready():
        for copy in copies:
            copy.wait()

    return ready


def blocks(count):
    return [slice(i, i + 256) for i in range(0, count, 256)]


def enc_first(pick, buf, w_embed, w_send, out, lat, sent, counts, embed, send, sems, *, chunks):
    copies = fetch(sems, (w_embed, embed), (w_send, send))
    band_sums(pick[0], buf, embed, send, lat, sent, counts, chunks, waits(copies))
    for here in blocks(out.shape[0]):
        out[here, :] = mm(counts[here, :], sent[...])


def enc_more(
    pick, buf, acc, w_embed, w_send, out, lat, sent, counts, embed, send, sems, *, chunks
):
    copies = fetch(sems, (w_embed, embed), (w_send, send))
    band_sums(pick[0], buf, embed, send, lat, sent, counts, chunks, waits(copies))
    for here in blocks(out.shape[0]):
        out[here, :] = acc[here, :] + mm(counts[here, :], sent[...])


def enc_last(
    pick,
    acc,
    gain,
    buf,
    w_embed,
    w_send,
    out,
    lat,
    sent,
    counts,
    embed,
    send,
    sems,
    load,
    load_sem,
    *,
    chunks,
):
    waits(fetch(load_sem, (buf, load)))()
    copies = fetch(sems, (w_embed, embed), (w_send, send))
    band_sums(pick[0], load, embed, send, lat, sent, counts, chunks, waits(copies))
    for here in blocks(out.shape[0]):
        summed = acc[here, :] + mm(counts[here, :], sent[...])
        out[here, :] = silu(rms(summed) * gain[...]).astype(jnp.bfloat16)


def node_update(node_in, w_node, init, out, node, init_here, sems):
    parts = blocks(out.shape[0])
    copies = fetch(
        sems, (w_node, node), *[(init.at[here, :], init_here.at[here, :]) for here in parts]
    )
    copies[0].wait()
    for i, here in enumerate(parts):
        fresh = mm(node_in[here, :], node[...])
        copies[1 + i].wait()
        out[here, :] = (init_here[here, :].astype(jnp.float32) + fresh).astype(jnp.bfloat16)


def sender_marks(pick, src, count, j):
    hot = []
    for i in range(4 * j, 4 * j + 4):
        code = src[i : i + 1, :]
        key = jnp.where(code // count == pick, code % count, -1)
        hot.append(hot_by_column(columns_of(key), count))
    return jnp.concatenate(hot, axis=0)


def proc_first(pick, src, nodes, out):
    for j in range(src.shape[0] // 4):
        hot = sender_marks(pick[0], src, nodes.shape[0], j)
        out[512 * j : 512 * (j + 1), :] = mm(hot, nodes[...]).astype(jnp.bfloat16)


def proc_more(pick, src, dst, nodes, acc, band_one, w_ps, w_pr, base, hot):
    count = nodes.shape[0]
    mine = LANES
    own = band_one[pl.ds(pl.multiple_of(pick[2] * mine, mine), mine), :]
    recv = mm(own, w_pr[...])
    top = recv.astype(jnp.bfloat16)
    rest = (recv - top.astype(jnp.float32)).astype(jnp.bfloat16)
    recv_pair = jnp.concatenate([top, rest], axis=0)
    for j in range(src.shape[0] // 4):
        at = slice(512 * j, 512 * (j + 1))
        near = mm(sender_marks(pick[0], src, count, j), nodes[...]).astype(jnp.bfloat16)
        recv_hot = []
        for i in range(4 * j, 4 * j + 4):
            one = hot_by_column(columns_of(dst[i : i + 1, :]), mine)
            recv_hot.append(side([one, one]))
        recv_rows = mm(jnp.concatenate(recv_hot, axis=0), recv_pair)
        base[at, :] = mm(acc[at, :] + near, w_ps[...]) + recv_rows
        hot[at, :] = sender_marks(pick[1], src, count, j)


def proc_last(pick, src, dst, nodes, base, hot, band_one, w_ps, w_po, w_ds, out, *, last_band):
    band, mine = pick[0], out.shape[0]
    band_nodes = nodes.shape[0]
    own = band_one[pl.ds(pl.multiple_of(pick[1] * mine, mine), mine), :]
    total = jnp.zeros(own.shape, jnp.float32)
    for j in range(src.shape[0] // 4):
        at = slice(512 * j, 512 * (j + 1))
        rows = mm(hot[at, :], nodes[...]).astype(jnp.bfloat16)
        back = []
        for i in range(4 * j, 4 * j + 4):
            target = band + src[i : i + 1, :] // band_nodes - 1
            valid = (target >= 0) & (target <= last_band)
            back.append(hot_by_row(jnp.where(valid, dst[i : i + 1, :], -1), mine))
        msg = silu(mm(rows, w_ps[...]) + base[at, :]).astype(jnp.bfloat16)
        total += mm(side(back), msg)
    norm = rms(total).astype(jnp.bfloat16)
    two = (own.astype(jnp.float32) + mm(norm, w_po[...])).astype(jnp.bfloat16)
    out[...] = silu(mm(two, w_ds[...])).astype(jnp.bfloat16)


def dec_counts(place, own, near, far, far_rest, out, held, sems, *, columns, skip, chunks):
    patches, _, grid_rows = own.shape
    patch, second = place[0], place[1]
    nodes = out.shape[1]
    half = far.shape[0]
    upper = patch >= half
    spot = jnp.where(upper, patch - half, patch)
    here = [own.at[patch], near.at[patch], far.at[spot], far_rest.at[spot]]
    waits(fetch(sems, *[(a, held.at[i]) for i, a in enumerate(here)]))()
    for k in range(3):
        count = skip + 3 * chunks
        notes = notes_of(held, k, columns, count)[skip:]
        if k == 2:
            later = notes_of(held, 3, columns, count)[skip:]
            notes = [jnp.where(upper, b, a) for a, b in zip(notes, later)]
        to, frm = [], []
        for j in range(chunks):
            high, low, dst = notes[j], notes[chunks + j], notes[2 * chunks + j]
            rel = (high % patches - patch) * (1 - 2 * second)
            turn = (rel + 2) & (patches - 1)
            spot = jnp.where(turn < 4, turn ^ 2, turn) ^ (3 * second)
            key = jnp.where(high // patches == place[2 + k], spot * LANES + low, -1)
            frm.append(key)
            to.append(dst)
        block = mm_nt(marks(to, grid_rows), marks(frm, nodes))
        out[grid_rows * k : grid_rows * (k + 1), :] = block.astype(jnp.bfloat16)


def dec_sums(counts, four, rest, out, *, first):
    half = four.shape[0]
    here = slice(first, first + out.shape[0])
    total = mm(counts[here, :half], four[...]) + mm(counts[here, half:], rest[...])
    out[...] = total.astype(out.dtype)


def dec_last(own, near, far, grid_vars, w_out, out):
    total = own[...] + near[...].astype(jnp.float32) + far[...].astype(jnp.float32)
    norm = rms(total).astype(jnp.bfloat16)
    fresh = grid_vars[...].astype(jnp.float32) + mm_nt(w_out[...], norm)
    out[...] = fresh.astype(jnp.bfloat16)


def call(body, out, *args, vmem=16, scalars=0, remote=0, scratch=(), flops=0, **static):
    block = pl.BlockSpec(memory_space=pltpu.VMEM)
    smem = pl.BlockSpec(memory_space=pltpu.SMEM)
    away = pl.BlockSpec(memory_space=pltpu.HBM)
    args = list(args)
    args[len(args) - remote :] = [
        pltpu.with_memory_space_constraint(a, pltpu.HBM) for a in args[len(args) - remote :]
    ]
    outs = out if isinstance(out, tuple) else (out,)
    moved = sum(a.size * a.dtype.itemsize for a in (*args, *outs))
    return pl.pallas_call(
        functools.partial(body, **static),
        out_shape=out,
        in_specs=[smem] * scalars + [block] * (len(args) - scalars - remote) + [away] * remote,
        out_specs=(block,) * len(out) if isinstance(out, tuple) else block,
        scratch_shapes=list(scratch),
        compiler_params=pltpu.CompilerParams(vmem_limit_bytes=vmem * MIB),
        cost_estimate=pl.CostEstimate(flops=flops, bytes_accessed=moved, transcendentals=0),
        name=body.__name__,
    )(*args)


def pair_groups(bands, patches, step):
    groups = []
    for b in range(bands):
        for p in range(patches):
            if (p + b) % 2 == 0:
                q = (p + 1) % patches if step == 0 else (p - 1) % patches
                groups.append([b * patches + p, b * patches + q])
    return groups


def shards(
    bands,
    patches,
    grid_vars,
    mesh_init,
    w_embed,
    w_send,
    w_node,
    node_gain,
    w_proc_send,
    w_proc_recv,
    w_proc_out,
    w_dec_send,
    w_dec_out,
    enc_src,
    enc_dst,
    proc_src,
    proc_dst,
    dec_src,
    dec_dst,
):
    f32, bf16 = jnp.float32, jnp.bfloat16
    shape = jax.ShapeDtypeStruct
    mine, width = mesh_init.shape
    band_nodes = patches * mine
    grid_rows, columns = grid_vars.shape
    edges = enc_src.shape[0]
    chunks = edges // LANES
    band = lax.axis_index("grid").astype(jnp.int32)
    patch = lax.axis_index("mesh").astype(jnp.int32)
    odd = band % 2
    far = 2 * odd
    near = 2 - far
    far_pairs = [(i, i + 1) for i in range(1, bands - 1, 2)]
    far_pairs += [(j, i) for i, j in far_pairs]
    near_pairs = [(i, i + 1) for i in range(0, bands - 1, 2)]
    near_pairs += [(j, i) for i, j in near_pairs]

    def over_far(block):
        return lax.ppermute(block, "grid", far_pairs)

    def over_near(block):
        return lax.ppermute(block, "grid", near_pairs)

    def scalars(*values):
        return jnp.stack(values).astype(jnp.int32)

    init_band = lax.all_gather(mesh_init, "mesh", axis=0, tiled=True)

    note_count = -(-(3 * edges + 3 * dec_src.size) // grid_rows)
    load_rows = -(-(columns + note_count) // 8) * 8
    grid_turned = grid_vars.T
    parts = [grid_turned]
    parts += [a.reshape(-1, LANES) for a in (enc_src, enc_dst, dec_src, dec_dst)]
    load = call(
        pack,
        shape((load_rows, grid_rows), bf16),
        *parts,
        remote=5,
        scratch=[pltpu.VMEM(a.shape, a.dtype) for a in parts] + [pltpu.SemaphoreType.DMA((5,))],
    )
    own = lax.all_gather(load, "mesh", axis=0, tiled=False)
    far_load = over_far(own[: patches // 2])
    far_after = over_far(own[patches // 2 :])
    near_load = over_near(own)

    band_rows = patches * grid_rows
    enc = dict(
        chunks=chunks,
        scalars=1,
        vmem=20,
        flops=band_rows * width,
    )
    def scratch(rows):
        return [
            pltpu.VMEM((rows, width), bf16),
            pltpu.VMEM((rows, width), bf16),
            pltpu.VMEM((band_nodes, rows), bf16),
            pltpu.VMEM((columns, width), bf16),
            pltpu.VMEM((width, width), bf16),
            pltpu.SemaphoreType.DMA((2,)),
        ]

    acc_shape = shape((band_nodes, width), f32)
    acc = call(
        enc_first, acc_shape, scalars(1), own, w_embed, w_send, remote=2, scratch=scratch(band_rows), **enc
    )
    acc = call(
        enc_more,
        acc_shape,
        scalars(2 - near),
        near_load,
        acc,
        w_embed,
        w_send,
        remote=2,
        scratch=scratch(band_rows),
        **enc,
    )
    acc = call(
        enc_more,
        acc_shape,
        scalars(2 - far),
        far_load,
        acc,
        w_embed,
        w_send,
        remote=2,
        scratch=scratch(band_rows // 2),
        **enc,
    )
    one_shape = shape((band_nodes, width), bf16)
    node_in = call(
        enc_last,
        one_shape,
        scalars(2 - far),
        acc,
        node_gain.reshape(1, width),
        far_after,
        w_embed,
        w_send,
        remote=3,
        scratch=scratch(band_rows // 2)
        + [pltpu.VMEM(far_after.shape, bf16), pltpu.SemaphoreType.DMA((1,))],
        **enc,
    )
    one = call(
        node_update,
        one_shape,
        node_in,
        w_node,
        init_band,
        remote=2,
        scratch=[
            pltpu.VMEM((width, width), bf16),
            pltpu.VMEM((band_nodes, width), bf16),
            pltpu.SemaphoreType.DMA((1 + band_nodes // 256,)),
        ],
    )

    far_one = over_far(one)
    near_one = over_near(one)
    src = proc_src.reshape(-1, LANES)
    dst = proc_dst.reshape(-1, LANES)
    proc_edges = proc_src.shape[0]
    pick = dict(scalars=1, flops=2 * proc_edges * band_nodes * width)
    pick_shape = shape((proc_edges, width), bf16)
    got = call(proc_first, pick_shape, scalars(1), src, one, **pick)

    second = (patch + band) % 2
    dec_edges = dec_src.shape[0]
    counts = call(
        dec_counts,
        shape((3 * grid_rows, band_nodes), bf16),
        scalars(patch, second, 1, 2 - near, 2 - far),
        own,
        near_load,
        far_load,
        far_after,
        scalars=1,
        remote=4,
        scratch=[pltpu.VMEM((4, load_rows, grid_rows), bf16), pltpu.SemaphoreType.DMA((4,))],
        flops=6 * grid_rows * band_nodes * dec_edges,
        columns=columns,
        skip=3 * chunks,
        chunks=dec_edges // LANES,
    )

    base, hot = call(
        proc_more,
        (shape((proc_edges, width), f32), shape((proc_edges, band_nodes), bf16)),
        scalars(near, far, patch),
        src,
        dst,
        near_one,
        got,
        one,
        w_proc_send,
        w_proc_recv,
        **pick,
    )
    sent = call(
        proc_last,
        shape((mine, width), bf16),
        scalars(band, patch),
        src,
        dst,
        far_one,
        base,
        hot,
        one,
        w_proc_send,
        w_proc_out,
        w_dec_send,
        last_band=bands - 1,
        **pick,
    )

    groups = [pair_groups(bands, patches, step) for step in (0, 1)]

    def meet(rows_here, step):
        return lax.all_gather(
            rows_here, ("grid", "mesh"), axis=0, tiled=True, axis_index_groups=groups[step]
        )

    def partner_half(both):
        size = both.shape[0] // 2
        return lax.dynamic_slice_in_dim(both, (1 - second) * size, size, 0)

    four = meet(meet(sent, 0), 1)
    rest = meet(partner_half(meet(partner_half(four), 0)), 1)
    flops = 2 * grid_rows * band_nodes * width
    part = shape((grid_rows, width), bf16)
    far_sums = over_far(call(dec_sums, part, counts, four, rest, flops=flops, first=2 * grid_rows))
    near_sums = over_near(call(dec_sums, part, counts, four, rest, flops=flops, first=grid_rows))
    own_sums = call(
        dec_sums, shape((grid_rows, width), f32), counts, four, rest, flops=flops, first=0
    )
    return call(
        dec_last,
        shape((columns, grid_rows), bf16),
        own_sums,
        near_sums,
        far_sums,
        grid_turned,
        w_dec_out.T,
        flops=flops,
    ).T


def solution(mesh):
    spread = P(("grid", "mesh"), None)
    edge = P(("grid", "mesh"))
    in_specs = (spread, spread) + (P(),) * 9 + (edge,) * 6
    body = functools.partial(shards, mesh.shape["grid"], mesh.shape["mesh"])
    return jax.shard_map(body, mesh=mesh, in_specs=in_specs, out_specs=spread, check_vma=False)
```

```python
import functools

import jax
import jax.numpy as jnp
from jax import lax
from jax.experimental import pallas as pl
from jax.experimental.pallas import tpu as pltpu
from jax.sharding import PartitionSpec as P

LANES = 128
MIB = 1024 * 1024


def silu(v):
    return v * (0.5 + 0.5 * jnp.tanh(0.5 * v))


def rms(v):
    return v * lax.rsqrt(jnp.mean(v * v, axis=-1, keepdims=True) + 1e-05)


def mm(a, b):
    return jnp.dot(a, b, preferred_element_type=jnp.float32)


def mm_tn(a, b):
    return lax.dot_general(a, b, (((0,), (0,)), ((), ())), preferred_element_type=jnp.float32)


def mm_nt(a, b):
    return lax.dot_general(a, b, (((1,), (1,)), ((), ())), preferred_element_type=jnp.float32)


def hot_by_row(keys, count):
    spots = lax.broadcasted_iota(jnp.int16, (count, keys.shape[1]), 0)
    one, none = jnp.bfloat16(1), jnp.bfloat16(0)
    return jnp.where(spots == keys.astype(jnp.int16), one, none)


def marks(rows, count):
    return side([hot_by_row(row, count).astype(jnp.float8_e4m3fn) for row in rows])


def columns_of(row):
    return jnp.transpose(jnp.broadcast_to(row, (LANES, LANES)))


def hot_by_column(spread, count):
    lanes = lax.broadcasted_iota(jnp.int32, (LANES, LANES), 1)
    parts = [
        jnp.where(spread == lanes + LANES * k, 1.0, 0.0).astype(jnp.bfloat16)
        for k in range(count // LANES)
    ]
    return jnp.concatenate(parts, axis=1)


def side(parts):
    return jnp.concatenate(parts, axis=1)


def notes_of(buf, s, columns, count):
    start = columns // 16 * 16
    notes = buf[s, start:, :].astype(jnp.float32).astype(jnp.int32)
    skip = columns - start

    def piece(k):
        row, lane = skip + k // 2, LANES * (k % 2)
        return notes[row : row + 1, lane : lane + LANES]

    return [piece(k) for k in range(count)]


def pack(*refs):
    out, sems = refs[5], refs[11]
    waits(fetch(sems, *zip(refs[:5], refs[6:11])))()
    grid_turned, enc_src, enc_dst, dec_src, dec_dst = refs[6:11]
    columns, grid_rows = grid_turned.shape
    start = columns // 16 * 16
    out[:start, :] = grid_turned[:start, :]
    pieces = []
    for part in (
        enc_src[...],
        enc_dst[...] // LANES,
        enc_dst[...] % LANES,
        dec_src[...] // LANES,
        dec_src[...] % LANES,
        dec_dst[...],
    ):
        part = part.astype(jnp.float32)
        pieces += [part[j : j + 1, :] for j in range(part.shape[0])]
    pieces += [jnp.zeros_like(pieces[0])] * (len(pieces) % 2)
    notes = [side(pieces[k : k + 2]) for k in range(0, len(pieces), 2)]
    blank = jnp.zeros((out.shape[0] - columns - len(notes), grid_rows), jnp.float32)
    rows = [grid_turned[start:, :].astype(jnp.float32)] + notes + [blank]
    out[start:, :] = jnp.concatenate(rows, axis=0).astype(jnp.bfloat16)


def fetch(sems, *pairs):
    copies = [pltpu.make_async_copy(a, b, sems.at[i]) for i, (a, b) in enumerate(pairs)]
    for copy in copies:
        copy.start()
    return copies


def band_sums(pick, buf, w_embed, w_send, lat, sent, counts, chunks, ready):
    patches, _, grid_rows = buf.shape
    columns = w_embed.shape[0]
    nodes = counts.shape[0]
    for s in range(patches):
        here = slice(grid_rows * s, grid_rows * (s + 1))
        notes = notes_of(buf, s, columns, 3 * chunks)
        to, frm = [], []
        for j in range(chunks):
            high, low = notes[chunks + j], notes[2 * chunks + j]
            key = jnp.where(high // patches == pick, (high % patches) * LANES + low, -1)
            to.append(key)
            frm.append(notes[j])
        counts[:, here] = mm_nt(marks(to, nodes), marks(frm, grid_rows)).astype(jnp.bfloat16)
    ready()
    for s in range(patches):
        here = slice(grid_rows * s, grid_rows * (s + 1))
        lat[here, :] = silu(mm_tn(buf[s, :columns, :], w_embed[...])).astype(jnp.bfloat16)
    for s in range(patches):
        here = slice(grid_rows * s, grid_rows * (s + 1))
        sent[here, :] = silu(mm(lat[here, :], w_send[...])).astype(jnp.bfloat16)


def waits(copies):
    def ready():
        for copy in copies:
            copy.wait()

    return ready


def blocks(count):
    return [slice(i, i + 256) for i in range(0, count, 256)]


def enc_first(pick, buf, w_embed, w_send, out, lat, sent, counts, embed, send, sems, *, chunks):
    copies = fetch(sems, (w_embed, embed), (w_send, send))
    band_sums(pick[0], buf, embed, send, lat, sent, counts, chunks, waits(copies))
    for here in blocks(out.shape[0]):
        out[here, :] = mm(counts[here, :], sent[...])


def enc_more(
    pick, buf, acc, w_embed, w_send, out, lat, sent, counts, embed, send, sems, *, chunks
):
    copies = fetch(sems, (w_embed, embed), (w_send, send))
    band_sums(pick[0], buf, embed, send, lat, sent, counts, chunks, waits(copies))
    for here in blocks(out.shape[0]):
        out[here, :] = acc[here, :] + mm(counts[here, :], sent[...])


def enc_last(
    pick, buf, acc, gain, w_embed, w_send, out, lat, sent, counts, embed, send, sems, *, chunks
):
    copies = fetch(sems, (w_embed, embed), (w_send, send))
    band_sums(pick[0], buf, embed, send, lat, sent, counts, chunks, waits(copies))
    for here in blocks(out.shape[0]):
        summed = acc[here, :] + mm(counts[here, :], sent[...])
        out[here, :] = silu(rms(summed) * gain[...]).astype(jnp.bfloat16)


def node_update(node_in, w_node, init, out, node, init_here, sems):
    parts = blocks(out.shape[0])
    copies = fetch(
        sems, (w_node, node), *[(init.at[here, :], init_here.at[here, :]) for here in parts]
    )
    copies[0].wait()
    for i, here in enumerate(parts):
        fresh = mm(node_in[here, :], node[...])
        copies[1 + i].wait()
        out[here, :] = (init_here[here, :].astype(jnp.float32) + fresh).astype(jnp.bfloat16)


def sender_marks(pick, src, count, j):
    hot = []
    for i in range(4 * j, 4 * j + 4):
        code = src[i : i + 1, :]
        key = jnp.where(code // count == pick, code % count, -1)
        hot.append(hot_by_column(columns_of(key), count))
    return jnp.concatenate(hot, axis=0)


def proc_first(pick, src, nodes, out):
    for j in range(src.shape[0] // 4):
        hot = sender_marks(pick[0], src, nodes.shape[0], j)
        out[512 * j : 512 * (j + 1), :] = mm(hot, nodes[...]).astype(jnp.bfloat16)


def proc_more(pick, src, dst, nodes, acc, band_one, w_ps, w_pr, base, hot):
    count = nodes.shape[0]
    mine = LANES
    own = band_one[pl.ds(pl.multiple_of(pick[2] * mine, mine), mine), :]
    recv = mm(own, w_pr[...])
    top = recv.astype(jnp.bfloat16)
    rest = (recv - top.astype(jnp.float32)).astype(jnp.bfloat16)
    recv_pair = jnp.concatenate([top, rest], axis=0)
    for j in range(src.shape[0] // 4):
        at = slice(512 * j, 512 * (j + 1))
        near = mm(sender_marks(pick[0], src, count, j), nodes[...]).astype(jnp.bfloat16)
        recv_hot = []
        for i in range(4 * j, 4 * j + 4):
            one = hot_by_column(columns_of(dst[i : i + 1, :]), mine)
            recv_hot.append(side([one, one]))
        recv_rows = mm(jnp.concatenate(recv_hot, axis=0), recv_pair)
        base[at, :] = mm(acc[at, :] + near, w_ps[...]) + recv_rows
        hot[at, :] = sender_marks(pick[1], src, count, j)


def proc_last(pick, src, dst, nodes, base, hot, band_one, w_ps, w_po, w_ds, out, *, last_band):
    band, mine = pick[0], out.shape[0]
    band_nodes = nodes.shape[0]
    own = band_one[pl.ds(pl.multiple_of(pick[1] * mine, mine), mine), :]
    total = jnp.zeros(own.shape, jnp.float32)
    for j in range(src.shape[0] // 4):
        at = slice(512 * j, 512 * (j + 1))
        rows = mm(hot[at, :], nodes[...]).astype(jnp.bfloat16)
        back = []
        for i in range(4 * j, 4 * j + 4):
            target = band + src[i : i + 1, :] // band_nodes - 1
            valid = (target >= 0) & (target <= last_band)
            back.append(hot_by_row(jnp.where(valid, dst[i : i + 1, :], -1), mine))
        msg = silu(mm(rows, w_ps[...]) + base[at, :]).astype(jnp.bfloat16)
        total += mm(side(back), msg)
    norm = rms(total).astype(jnp.bfloat16)
    two = (own.astype(jnp.float32) + mm(norm, w_po[...])).astype(jnp.bfloat16)
    out[...] = silu(mm(two, w_ds[...])).astype(jnp.bfloat16)


def dec_counts(place, own, near, far, out, *, columns, skip, chunks):
    patches, _, grid_rows = own.shape
    patch, second = place[0], place[1]
    nodes = out.shape[1]
    for k, buf in enumerate((own, near, far)):
        notes = notes_of(buf, patch, columns, skip + 3 * chunks)[skip:]
        to, frm = [], []
        for j in range(chunks):
            high, low, dst = notes[j], notes[chunks + j], notes[2 * chunks + j]
            rel = (high % patches - patch) * (1 - 2 * second)
            turn = (rel + 2) & (patches - 1)
            spot = jnp.where(turn < 4, turn ^ 2, turn) ^ (3 * second)
            key = jnp.where(high // patches == place[2 + k], spot * LANES + low, -1)
            frm.append(key)
            to.append(dst)
        block = mm_nt(marks(to, grid_rows), marks(frm, nodes))
        out[grid_rows * k : grid_rows * (k + 1), :] = block.astype(jnp.bfloat16)


def dec_sums(counts, four, rest, out, *, first):
    half = four.shape[0]
    here = slice(first, first + out.shape[0])
    total = mm(counts[here, :half], four[...]) + mm(counts[here, half:], rest[...])
    out[...] = total.astype(out.dtype)


def dec_last(own, far, near, grid_vars, w_out, out):
    total = own[...] + near[...].astype(jnp.float32) + far[...].astype(jnp.float32)
    norm = rms(total).astype(jnp.bfloat16)
    fresh = grid_vars[...].astype(jnp.float32) + mm_nt(w_out[...], norm)
    out[...] = fresh.astype(jnp.bfloat16)


def call(body, out, *args, vmem=16, scalars=0, remote=0, scratch=(), flops=0, **static):
    block = pl.BlockSpec(memory_space=pltpu.VMEM)
    smem = pl.BlockSpec(memory_space=pltpu.SMEM)
    away = pl.BlockSpec(memory_space=pltpu.HBM)
    args = list(args)
    args[len(args) - remote :] = [
        pltpu.with_memory_space_constraint(a, pltpu.HBM) for a in args[len(args) - remote :]
    ]
    outs = out if isinstance(out, tuple) else (out,)
    moved = sum(a.size * a.dtype.itemsize for a in (*args, *outs))
    return pl.pallas_call(
        functools.partial(body, **static),
        out_shape=out,
        in_specs=[smem] * scalars + [block] * (len(args) - scalars - remote) + [away] * remote,
        out_specs=(block,) * len(out) if isinstance(out, tuple) else block,
        scratch_shapes=list(scratch),
        compiler_params=pltpu.CompilerParams(vmem_limit_bytes=vmem * MIB),
        cost_estimate=pl.CostEstimate(flops=flops, bytes_accessed=moved, transcendentals=0),
        name=body.__name__,
    )(*args)


def pair_groups(bands, patches, step):
    groups = []
    for b in range(bands):
        for p in range(patches):
            if (p + b) % 2 == 0:
                q = (p + 1) % patches if step == 0 else (p - 1) % patches
                groups.append([b * patches + p, b * patches + q])
    return groups


def shards(
    bands,
    patches,
    grid_vars,
    mesh_init,
    w_embed,
    w_send,
    w_node,
    node_gain,
    w_proc_send,
    w_proc_recv,
    w_proc_out,
    w_dec_send,
    w_dec_out,
    enc_src,
    enc_dst,
    proc_src,
    proc_dst,
    dec_src,
    dec_dst,
):
    f32, bf16 = jnp.float32, jnp.bfloat16
    shape = jax.ShapeDtypeStruct
    mine, width = mesh_init.shape
    band_nodes = patches * mine
    grid_rows, columns = grid_vars.shape
    edges = enc_src.shape[0]
    chunks = edges // LANES
    band = lax.axis_index("grid").astype(jnp.int32)
    patch = lax.axis_index("mesh").astype(jnp.int32)
    odd = band % 2
    far = 2 * odd
    near = 2 - far
    far_pairs = [(i, i + 1) for i in range(1, bands - 1, 2)]
    far_pairs += [(j, i) for i, j in far_pairs]
    near_pairs = [(i, i + 1) for i in range(0, bands - 1, 2)]
    near_pairs += [(j, i) for i, j in near_pairs]

    def over_far(block):
        return lax.ppermute(block, "grid", far_pairs)

    def over_near(block):
        return lax.ppermute(block, "grid", near_pairs)

    def scalars(*values):
        return jnp.stack(values).astype(jnp.int32)

    init_band = lax.all_gather(mesh_init, "mesh", axis=0, tiled=True)

    note_count = -(-(3 * edges + 3 * dec_src.size) // grid_rows)
    load_rows = -(-(columns + note_count) // 8) * 8
    grid_turned = grid_vars.T
    parts = [grid_turned]
    parts += [a.reshape(-1, LANES) for a in (enc_src, enc_dst, dec_src, dec_dst)]
    load = call(
        pack,
        shape((load_rows, grid_rows), bf16),
        *parts,
        remote=5,
        scratch=[pltpu.VMEM(a.shape, a.dtype) for a in parts] + [pltpu.SemaphoreType.DMA((5,))],
    )
    own = lax.all_gather(load, "mesh", axis=0, tiled=False)
    far_load = over_far(own)
    near_load = over_near(own)

    band_rows = patches * grid_rows
    enc = dict(
        chunks=chunks,
        scalars=1,
        vmem=20,
        flops=band_rows * width,
    )
    scratch = [
        pltpu.VMEM((band_rows, width), bf16),
        pltpu.VMEM((band_rows, width), bf16),
        pltpu.VMEM((band_nodes, band_rows), bf16),
        pltpu.VMEM((columns, width), bf16),
        pltpu.VMEM((width, width), bf16),
        pltpu.SemaphoreType.DMA((2,)),
    ]
    acc_shape = shape((band_nodes, width), f32)
    acc = call(
        enc_first, acc_shape, scalars(1), own, w_embed, w_send, remote=2, scratch=scratch, **enc
    )
    acc = call(
        enc_more,
        acc_shape,
        scalars(2 - near),
        near_load,
        acc,
        w_embed,
        w_send,
        remote=2,
        scratch=scratch,
        **enc,
    )
    one_shape = shape((band_nodes, width), bf16)
    node_in = call(
        enc_last,
        one_shape,
        scalars(2 - far),
        far_load,
        acc,
        node_gain.reshape(1, width),
        w_embed,
        w_send,
        remote=2,
        scratch=scratch,
        **enc,
    )
    one = call(
        node_update,
        one_shape,
        node_in,
        w_node,
        init_band,
        remote=2,
        scratch=[
            pltpu.VMEM((width, width), bf16),
            pltpu.VMEM((band_nodes, width), bf16),
            pltpu.SemaphoreType.DMA((1 + band_nodes // 256,)),
        ],
    )

    far_one = over_far(one)
    near_one = over_near(one)
    src = proc_src.reshape(-1, LANES)
    dst = proc_dst.reshape(-1, LANES)
    proc_edges = proc_src.shape[0]
    pick = dict(scalars=1, flops=2 * proc_edges * band_nodes * width)
    pick_shape = shape((proc_edges, width), bf16)
    got = call(proc_first, pick_shape, scalars(1), src, one, **pick)

    second = (patch + band) % 2
    dec_edges = dec_src.shape[0]
    counts = call(
        dec_counts,
        shape((3 * grid_rows, band_nodes), bf16),
        scalars(patch, second, 1, 2 - near, 2 - far),
        own,
        near_load,
        far_load,
        scalars=1,
        flops=6 * grid_rows * band_nodes * dec_edges,
        columns=columns,
        skip=3 * chunks,
        chunks=dec_edges // LANES,
    )

    base, hot = call(
        proc_more,
        (shape((proc_edges, width), f32), shape((proc_edges, band_nodes), bf16)),
        scalars(near, far, patch),
        src,
        dst,
        near_one,
        got,
        one,
        w_proc_send,
        w_proc_recv,
        **pick,
    )
    sent = call(
        proc_last,
        shape((mine, width), bf16),
        scalars(band, patch),
        src,
        dst,
        far_one,
        base,
        hot,
        one,
        w_proc_send,
        w_proc_out,
        w_dec_send,
        last_band=bands - 1,
        **pick,
    )

    groups = [pair_groups(bands, patches, step) for step in (0, 1)]

    def meet(rows_here, step):
        return lax.all_gather(
            rows_here, ("grid", "mesh"), axis=0, tiled=True, axis_index_groups=groups[step]
        )

    def partner_half(both):
        size = both.shape[0] // 2
        return lax.dynamic_slice_in_dim(both, (1 - second) * size, size, 0)

    four = meet(meet(sent, 0), 1)
    rest = meet(partner_half(meet(partner_half(four), 0)), 1)
    flops = 2 * grid_rows * band_nodes * width
    part = shape((grid_rows, width), bf16)
    far_sums = over_far(call(dec_sums, part, counts, four, rest, flops=flops, first=2 * grid_rows))
    near_sums = over_near(call(dec_sums, part, counts, four, rest, flops=flops, first=grid_rows))
    own_sums = call(
        dec_sums, shape((grid_rows, width), f32), counts, four, rest, flops=flops, first=0
    )
    return call(
        dec_last,
        shape((columns, grid_rows), bf16),
        own_sums,
        far_sums,
        near_sums,
        grid_turned,
        w_dec_out.T,
        flops=flops,
    ).T


def solution(mesh):
    spread = P(("grid", "mesh"), None)
    edge = P(("grid", "mesh"))
    in_specs = (spread, spread) + (P(),) * 9 + (edge,) * 6
    body = functools.partial(shards, mesh.shape["grid"], mesh.shape["mesh"])
    return jax.shard_map(body, mesh=mesh, in_specs=in_specs, out_specs=spread, check_vma=False)
```
